256 devices in a mesh: panel: 2 (over z_lo), tile: 32 (over z_hi, y, core), rad: 4 (over x).
Axes of the slice: x: 4, y: 4, z: 8 (z_hi: 4, z_lo: 2; z = z_hi * 2 + z_lo), core: 2. Of those that a mesh axis runs over, the one named last changes fastest.
Arguments:
- state: float32 [2, 8, 32, 1024, 512], P('panel', None, 'rad', 'tile'), may hold values from -2.5 to 2.5
- donor_base: int32 [2, 32, 32, 4], P('panel', 'tile'), may hold values from 0 to 15870, as said below
- fractions: float32 [2, 32, 2, 32, 4], P('panel', 'tile'), may hold values from 0 to 1
- dest_pos: int32 [2, 32, 32, 4], P('panel', 'tile'), may hold values from 0 to 127, as said below
Outputs:
- new_state: float32 [2, 8, 32, 1024, 512], P('panel', None, 'rad', 'tile')
The draws below stay inside these ranges and needn't reach their ends.
Inputs may be any that keep to these rules, and one draw needn't show every extreme that they name: `donor_base`: each entry is phi * 512 + theta with phi below 31 and theta below 511, so that all four stencil cells lie in the donor tile. `dest_pos`: for each panel and tile, the 32 x 4 entries name every border point 0 to 127 exactly once.
All inputs are finite; a program needn't handle non-finite values.
Results may differ from the reference program's by a relative error of at most 0.00005.
Values sent between devices are 32-bit elements; how exact they have to be, the bound alone decides.
No kernel may reach another device: no remote copies, remote signals or barrier semaphores. Data moves between devices by JAX's collectives and lax.ppermute only.
A program may use at most 128 MiB of HBM per device.

```python
import math
import jax
import jax.numpy as jnp
from jax import lax

NTH = 512
CP = 32
TILES = 32
NP = 1024
NR = 32
NB = 128
SLOTS = 4


def draw_donor_base(key, part):
    key = jax.random.fold_in(key, 11)
    key_phi, key_theta = jax.random.split(key)
    column = jax.random.randint(key_phi, (2, TILES, TILES, SLOTS), 0, CP - 1)
    row = jax.random.randint(key_theta, (2, TILES, TILES, SLOTS), 0, NTH - 1)
    cells = column * NTH + row
    cells = cells.at[0, 0, 0, 0].set((CP - 1) * NTH - 2)
    cells = cells.at[0, 0, 1, 0].set(0)
    return cells.astype(jnp.int32)


def draw_dest_pos(key, part):
    key = jax.random.fold_in(key, 12)
    keys = jax.random.split(key, 2 * TILES)
    orders = jax.vmap(lambda single: jax.random.permutation(single, NB))(keys)
    return orders.reshape(2, TILES, TILES, SLOTS).astype(jnp.int32)


def block_scale(stream_key, extent, shards, low, largest):
    level = 1.0
    for axis_at, parts in shards:
        steps = jax.random.uniform(jax.random.fold_in(jax.random.fold_in(stream_key, 6), axis_at), (parts,), jnp.float32, low / len(shards), largest / len(shards))
        level = level * jnp.repeat(jnp.exp(steps), extent[axis_at] // parts).reshape((-1,) + (1,) * (len(extent) - 1 - axis_at))
    return level


def noise(stream_key, extent, spread, most, shards=(), held_as=jnp.bfloat16):
    array = jax.random.normal(stream_key, extent, jnp.float32) * spread
    if len(shards) > 0:
        array = block_scale(stream_key, extent, shards, -0.22, 0.18) * array
    return jnp.clip(array, min=-most, max=most).astype(held_as)


def setup_inputs(seed: int = 0) -> dict:
    streams_of = jax.random.split(jax.random.key(seed), 5)
    return {
        "state": noise(streams_of[0], (2, 8, NR, NP, NTH), 0.5, 2.5, ((0, 2), (2, 4), (3, 32)), jnp.float32),
        "donor_base": draw_donor_base(jax.random.fold_in(streams_of[4], 71), 0),
        "fractions": jnp.clip(1.0 * jax.random.uniform(streams_of[2], (2, TILES, 2, TILES, SLOTS), jnp.float32) ** block_scale(streams_of[2], (2, TILES, 2, TILES, SLOTS), ((0, 2), (1, 32)), -0.2, 0.2), 0.0, 1.0),
        "dest_pos": draw_dest_pos(jax.random.fold_in(streams_of[4], 71), 0),
    }


BASE_RADIUS = 0.6


def geometry(theta_count, phi_count):
    theta_step = 0.5 * math.pi / theta_count
    phi_step = 1.5 * math.pi / phi_count
    shell_step = 0.6 * min(theta_step, phi_step)
    corner = BASE_RADIUS * math.sin(0.25 * math.pi)
    spacing = min(shell_step, corner * theta_step, corner * phi_step)
    return theta_step, phi_step, shell_step, spacing


def first_four(padded, axis, length):
    def piece(offset):
        return lax.slice_in_dim(padded, offset, offset + length, axis=axis)
    return (piece(0) - 8.0 * piece(1) + 8.0 * piece(3) - piece(4)) / 12.0


def second_four(padded, axis, length):
    def piece(offset):
        return lax.slice_in_dim(padded, offset, offset + length, axis=axis)
    return (-piece(0) + 16.0 * piece(1) - 30.0 * piece(2) + 16.0 * piece(3) - piece(4)) / 12.0


def section_update(center, phi_padded, shell_padded, radius, colat, theta_step, phi_step, shell_step, spacing):
    shells = center.shape[1]
    cols = center.shape[2]
    rows = center.shape[3]
    theta_padded = jnp.pad(center, ((0, 0), (0, 0), (0, 0), (2, 2)))
    inner = lax.slice_in_dim(shell_padded, 0, shells, axis=1)
    outer = lax.slice_in_dim(shell_padded, 2, shells + 2, axis=1)
    grad_shell = (outer - inner) * (0.5 / shell_step)
    lap_shell = (outer - 2.0 * center + inner) * (1.0 / (shell_step * shell_step))
    theta_scale = (1.0 / (radius * theta_step)).reshape(1, shells, 1, 1)
    phi_scale = (1.0 / (radius[:, None] * jnp.sin(colat)[None, :] * phi_step)).reshape(1, shells, 1, rows)
    grad_theta = first_four(theta_padded, 3, rows) * theta_scale
    grad_phi = first_four(phi_padded, 2, cols) * phi_scale
    laplace = lap_shell + second_four(theta_padded, 3, rows) * (theta_scale * theta_scale)
    laplace = laplace + second_four(phi_padded, 2, cols) * (phi_scale * phi_scale)
    lnrho = center[0]
    velocity = center[1:4]
    magnetic = center[4:7]
    pressure = center[7]
    advect = velocity[0] * grad_shell + velocity[1] * grad_theta + velocity[2] * grad_phi
    along_field = magnetic[0] * grad_shell + magnetic[1] * grad_theta + magnetic[2] * grad_phi
    diverge = grad_shell[1] + grad_theta[2] + grad_phi[3]
    inv_rho = jnp.exp(-lnrho)
    grad_press = jnp.stack([grad_shell[7], grad_theta[7], grad_phi[7]])
    rate_rho = -advect[0] - diverge
    rate_vel = -advect[1:4] - inv_rho * grad_press + inv_rho * along_field[4:7] + (0.25 * spacing) * laplace[1:4]
    rate_mag = -advect[4:7] + along_field[1:4] - magnetic * diverge + (0.2 * spacing) * laplace[4:7]
    rate_press = -advect[7] - (5.0 / 3.0) * pressure * diverge + (0.3 * spacing) * laplace[7]
    rates = jnp.concatenate([rate_rho[None], rate_vel, rate_mag, rate_press[None]], axis=0)
    return center + (0.2 * spacing) * rates


def fill_panel(receiver, donor, donor_base, fractions, dest_pos):
    count, shells, phis, rows = receiver.shape
    tiles = donor_base.shape[0]
    width = phis // tiles
    flat = donor.reshape(count, shells, phis * rows)
    base = jnp.transpose(donor_base, (1, 0, 2))
    start = (jnp.arange(tiles, dtype=jnp.int32) * (width * rows))[None, :, None] + base
    frac_theta = jnp.transpose(fractions[:, 0], (1, 0, 2))
    frac_phi = jnp.transpose(fractions[:, 1], (1, 0, 2))
    weights = ((1.0 - frac_phi) * (1.0 - frac_theta), (1.0 - frac_phi) * frac_theta,
               frac_phi * (1.0 - frac_theta), frac_phi * frac_theta)
    offsets = (0, 1, rows, rows + 1)
    terms = [flat[:, :, start + offset] * weight for offset, weight in zip(offsets, weights)]
    values = ((terms[0] + terms[1]) + terms[2]) + terms[3]
    tile_index = jnp.broadcast_to(jnp.arange(tiles, dtype=jnp.int32)[:, None, None], dest_pos.shape)
    border = jnp.zeros((count, shells, tiles, 4 * width), jnp.float32)
    border = border.at[:, :, tile_index, dest_pos].set(values)
    border = border.reshape(count, shells, tiles, 4, width)
    border = jnp.transpose(border, (0, 1, 2, 4, 3)).reshape(count, shells, phis, 4)
    filled = receiver.at[:, :, :, 0:2].set(border[..., 0:2])
    return filled.at[:, :, :, rows - 2:].set(border[..., 2:4])


def reference(state, donor_base, fractions, dest_pos):
    theta_step, phi_step, shell_step, spacing = geometry(NTH, NP)
    colat = 0.25 * math.pi + (jnp.arange(NTH, dtype=jnp.int32).astype(jnp.float32) + 0.5) * theta_step
    radius_all = BASE_RADIUS + (jnp.arange(NR, dtype=jnp.int32).astype(jnp.float32) + 0.5) * shell_step
    panels = []
    for side in range(2):
        filled = fill_panel(state[side], state[1 - side], donor_base[1 - side], fractions[1 - side], dest_pos[side])
        phi_pad = jnp.pad(filled, ((0, 0), (0, 0), (2, 2), (0, 0)))
        shell_pad = jnp.pad(filled, ((0, 0), (1, 1), (0, 0), (0, 0)))

        def one_shell(layer):
            center = lax.dynamic_slice_in_dim(filled, layer, 1, 1)
            phi_part = lax.dynamic_slice_in_dim(phi_pad, layer, 1, 1)
            shell_part = lax.dynamic_slice_in_dim(shell_pad, layer, 3, 1)
            radius = lax.dynamic_slice_in_dim(radius_all, layer, 1, 0)
            return section_update(center, phi_part, shell_part, radius, colat,
                                theta_step, phi_step, shell_step, spacing)[:, 0]

        result = lax.map(one_shell, jnp.arange(NR, dtype=jnp.int32))
        panels.append(jnp.transpose(result, (1, 0, 2, 3)))
    return jnp.stack(panels)
```

```python
import functools
import math

import jax
import jax.numpy as jnp
import numpy as np
from jax import lax
from jax.experimental import pallas as pl
from jax.experimental.pallas import tpu as pltpu
from jax.sharding import PartitionSpec as P

BASE_RADIUS = 0.6
F32 = jnp.float32
BF16 = jnp.bfloat16
LANES = 128
FIRST = 8
ROWS = 48


def geometry(theta_count, phi_count):
    theta_step = 0.5 * math.pi / theta_count
    phi_step = 1.5 * math.pi / phi_count
    shell_step = 0.6 * min(theta_step, phi_step)
    corner = BASE_RADIUS * math.sin(0.25 * math.pi)
    spacing = min(shell_step, corner * theta_step, corner * phi_step)
    return (theta_step, phi_step, shell_step, spacing)


def halves(x):
    high = x.astype(BF16)
    return high, (x - high.astype(F32)).astype(BF16)


def lane_order(table):
    tiles = table.shape[0]
    lane = lax.broadcasted_iota(jnp.int32, (tiles, LANES), 1)
    row = lax.broadcasted_iota(jnp.int32, (tiles, LANES), 0)
    slot = 2 * (lane // 64) + lane % 2
    wide = jnp.zeros((tiles, LANES), F32)
    for s in range(4):
        wide = jnp.where(slot == s, table[:, s : s + 1], wide)
    wide = jnp.where((lane % 64) // 2 == row, wide, 0.0)
    return jnp.sum(wide, axis=0, keepdims=True)


def payload_kernel(
    panel_ref, x_ref, base_ref, frac_ref, pay_ref, cols_ref, held, values, load_sem, cols_sem
):
    stacked, cols, rows = held.shape
    chunk = 8
    chunks = stacked // chunk

    def load(i):
        part = pl.ds(i * chunk, chunk)
        return pltpu.make_async_copy(x_ref.at[part], held.at[part], load_sem.at[i])

    def column(k, c):
        return pltpu.make_async_copy(x_ref.at[:, c, :], cols_ref.at[k], cols_sem.at[k])

    edges = ((0, 0), (1, 1), (2, cols - 2), (3, cols - 1))
    for i in range(chunks):
        load(i).start()
    for k, c in edges:
        column(k, c).start()
    base = lane_order(base_ref[...].astype(F32)).astype(jnp.int32)
    frac_theta = lane_order(frac_ref[0])
    frac_phi = lane_order(frac_ref[1])
    phi = base // rows
    theta = base - phi * rows
    position = lax.broadcasted_iota(jnp.int32, (rows, LANES), 0)
    along_theta = jnp.where(position == theta, 1.0 - frac_theta, 0.0)
    along_theta = along_theta + jnp.where(position == theta + 1, frac_theta, 0.0)
    high, low = halves(along_theta)
    both = jnp.concatenate([high, low], axis=1)
    place = lax.broadcasted_iota(jnp.int32, (cols, LANES), 0)
    along_phi = jnp.where(place == phi, 1.0 - frac_phi, 0.0)
    along_phi = along_phi + jnp.where(place == phi + 1, frac_phi, 0.0)
    for i in range(chunks):
        load(i).wait()
        x_high, x_low = halves(held[i * chunk : (i + 1) * chunk].reshape(chunk * cols, rows))
        wide = jnp.dot(x_high, both, preferred_element_type=F32)
        line = wide[:, :LANES] + wide[:, LANES:] + jnp.dot(x_low, high, preferred_element_type=F32)
        line = line.reshape(chunk, cols, LANES) * along_phi[None]
        values[i * chunk : (i + 1) * chunk, :] = jnp.sum(line, axis=1)
    found = values[...]
    folded = jnp.concatenate([found, pltpu.roll(found, 64, axis=1)], axis=0)
    pay_ref[...] = jnp.zeros(pay_ref.shape, F32)
    start = pl.multiple_of((1 - panel_ref[0]) * 64, 64)
    pay_ref[pl.ds(start, 64), :] = jnp.transpose(folded)[:64, :]
    for k, c in edges:
        column(k, c).wait()


def payload_call(panel, x, base, fractions):
    stacked, cols, rows = x.shape
    tiles = base.shape[0]
    vmem = pl.BlockSpec(memory_space=pltpu.VMEM)
    anywhere = pl.BlockSpec(memory_space=pl.ANY)
    return pl.pallas_call(
        payload_kernel,
        out_shape=(
            jax.ShapeDtypeStruct((4 * tiles, LANES), F32),
            jax.ShapeDtypeStruct((4, stacked, rows), F32),
        ),
        in_specs=[pl.BlockSpec(memory_space=pltpu.SMEM), anywhere, vmem, vmem],
        out_specs=(vmem, anywhere),
        scratch_shapes=[
            pltpu.VMEM((stacked, cols, rows), F32),
            pltpu.VMEM((stacked, LANES), F32),
            pltpu.SemaphoreType.DMA((8,)),
            pltpu.SemaphoreType.DMA((4,)),
        ],
        compiler_params=pltpu.CompilerParams(vmem_limit_bytes=32 * 2**20),
        cost_estimate=pl.CostEstimate(flops=10**9, bytes_accessed=6 * 2**20, transcendentals=0),
        name="payload",
    )(panel, x, base, fractions)


def place_kernel(panel_ref, got_ref, dest_ref, border_ref):
    start = pl.multiple_of((1 - panel_ref[0]) * 64, 64)
    got = got_ref[pl.ds(start, 64), :]
    turned = jnp.transpose(jnp.concatenate([got, got], axis=0))
    lane = lax.broadcasted_iota(jnp.int32, (64, LANES), 1)
    values = jnp.where(lane < 64, turned[:64], turned[64:])
    point = lane_order(dest_ref[...].astype(F32)).astype(jnp.int32)
    placing = jnp.where(
        lax.broadcasted_iota(jnp.int32, (LANES, LANES), 0) == point, 1.0, 0.0
    ).astype(BF16)
    dims = (((1,), (1,)), ((), ()))
    high, low = halves(values)
    border = lax.dot_general(high, placing, dims, preferred_element_type=F32)
    border_ref[...] = border + lax.dot_general(low, placing, dims, preferred_element_type=F32)


def place_call(panel, got, dest):
    vmem = pl.BlockSpec(memory_space=pltpu.VMEM)
    return pl.pallas_call(
        place_kernel,
        out_shape=jax.ShapeDtypeStruct((64, LANES), F32),
        in_specs=[pl.BlockSpec(memory_space=pltpu.SMEM), vmem, vmem],
        out_specs=vmem,
        cost_estimate=pl.CostEstimate(flops=10**7, bytes_accessed=2**17, transcendentals=0),
        name="place",
    )(panel, got, dest)


def section_chunk(load, scale, lane):
    a_r, a_t, a_p, c_r, c_t, c_p = scale
    c_mid = 2.0 * c_r + 30.0 * c_t + 30.0 * c_p

    def parts(f, laplace=True):
        x = load(f, 0, 0, 0)
        left, right = load(f, 0, 0, -1), load(f, 0, 0, 1)
        inner, outer = load(f, -1, 0, 0), load(f, 1, 0, 0)
        t1 = pltpu.roll(jnp.where(lane < 1, right, x), LANES - 1, axis=1)
        t2 = pltpu.roll(jnp.where(lane < 2, right, x), LANES - 2, axis=1)
        s1 = pltpu.roll(jnp.where(lane >= LANES - 1, left, x), 1, axis=1)
        s2 = pltpu.roll(jnp.where(lane >= LANES - 2, left, x), 2, axis=1)
        p1, p2 = load(f, 0, 1, 0), load(f, 0, 2, 0)
        q1, q2 = load(f, 0, -1, 0), load(f, 0, -2, 0)
        g_r = outer - inner
        g_t = 8.0 * (t1 - s1) - (t2 - s2)
        g_p = 8.0 * (p1 - q1) - (p2 - q2)
        if not laplace:
            return x, g_r, g_t, g_p, None
        lap = c_r * (outer + inner) + c_t * (16.0 * (t1 + s1) - (t2 + s2))
        lap = lap + c_p * (16.0 * (p1 + q1) - (p2 + q2)) - c_mid * x
        return x, g_r, g_t, g_p, lap

    vel = tuple(load(1 + i, 0, 0, 0) * a for i, a in enumerate((a_r, a_t, a_p)))
    mag = tuple(load(4 + i, 0, 0, 0) * a for i, a in enumerate((a_r, a_t, a_p)))

    def along(v, g):
        return v[0] * g[0] + v[1] * g[1] + v[2] * g[2]

    new = [None] * 8
    rho, *g_rho, _ = parts(0, laplace=False)
    inv_rho = jnp.exp(-rho)
    rho_adv = along(vel, g_rho)
    pres, *g_pres, lap = parts(7)
    part_pres = pres - along(vel, g_pres) + 0.3 * lap
    div = None
    part_mag = []
    for i, a in enumerate((a_r, a_t, a_p)):
        u, *g_u, lap_u = parts(1 + i)
        b, *g_b, lap_b = parts(4 + i)
        term = a * g_u[i]
        div = term if div is None else div + term
        force = along(mag, g_b) - a * g_pres[i]
        new[1 + i] = u - along(vel, g_u) + inv_rho * force + 0.25 * lap_u
        part_mag.append((b, b - along(vel, g_b) + along(mag, g_u) + 0.2 * lap_b))
    for i, (b, part) in enumerate(part_mag):
        new[4 + i] = part - b * div
    new[0] = rho - rho_adv - div
    new[7] = part_pres - (5.0 / 3.0) * pres * div
    return new


def section_kernel(tiles_here, merge, shells, cols, rows, phi_count, *refs):
    if merge:
        inverse_ref, sine_ref, x_ref, below_ref, above_ref, before_ref, after_ref, *refs = refs
        own_ref, low_ref, high_ref, left_ref, right_ref, _, out_ref, *refs = refs
        held, made, split, spread, in_sem, halo_sem, out_sem = refs
    else:
        inverse_ref, sine_ref, x_ref, below_ref, above_ref, before_ref, after_ref, *refs = refs
        out_ref, held, made, in_sem, halo_sem, out_sem = refs
    lane_tiles = rows // LANES
    fields = 8
    theta_step, phi_step, shell_step, spacing = geometry(rows, phi_count)
    step = 0.2 * spacing

    def loads(s, k):
        lanes = pl.ds(k * LANES, LANES)
        if isinstance(s, int) and s == -1:
            source = below_ref.at[:, :, lanes]
        elif isinstance(s, int) and s == shells:
            source = above_ref.at[:, :, lanes]
        else:
            source = x_ref.at[:, s, :, lanes]
        target = held.at[k, :, s + 1, pl.ds(FIRST, cols), :]
        return pltpu.make_async_copy(source, target, in_sem.at[s + 1, k])

    def halo(side, c, k):
        source = (before_ref, after_ref)[side]
        row = (FIRST - 2, FIRST + cols)[side] + c
        return pltpu.make_async_copy(
            source.at[c, :, :, pl.ds(k * LANES, LANES)],
            held.at[k, :, pl.ds(1, shells), row, :],
            halo_sem.at[side, c, k],
        )

    def store(s, n, k):
        return pltpu.make_async_copy(
            made.at[n, s], out_ref.at[:, s, :, pl.ds(k * LANES, LANES)], out_sem.at[n, s]
        )

    halos = [(side, c, k) for side in range(2) for c in range(2) for k in tiles_here]
    for h in halos:
        halo(*h).start()
    for s in range(-1, shells + 1):
        for k in range(lane_tiles):
            loads(s, k).start()

    lane = lax.broadcasted_iota(jnp.int32, (8, LANES), 1)

    if merge:
        for n, ref in enumerate((own_ref, low_ref, high_ref, left_ref, right_ref)):
            value = ref[...]
            high = value.astype(BF16).astype(F32)
            split[n, 0] = high
            split[n, 1] = value - high
        wide = lax.broadcasted_iota(jnp.int32, (LANES, LANES), 1)
        group = lax.broadcasted_iota(jnp.int32, (LANES, LANES), 0) // cols
        target = jnp.where(group < 2, group, LANES - 4 + group)
        spreading = jnp.where(wide == target, 1.0, 0.0).astype(BF16)
        row = lax.broadcasted_iota(jnp.int32, (8, LANES), 0)
        within = lane % cols

        def spread_rows(part, s, f, r, inside):
            index = pl.ds(f * shells + s, 1)
            if not inside:
                which = 1 if inside is None else 2
                return jnp.where(within == row + (8 * r - FIRST), split[which, part, index, :], 0.0)
            if r == 0:
                wanted, which = (row >= 6) & (within == row + (cols - 8)), 3
            elif r == ROWS // 8 - 1:
                wanted, which = (row < 2) & (within == row), 4
            else:
                wanted, which = within == row + (8 * r - FIRST), 0
            return jnp.where(wanted, split[which, part, index, :], 0.0)

        def merge_shell(slot, s, inside):
            tiles = range(ROWS // 8) if inside else range(1, ROWS // 8 - 1)
            for f in range(fields):
                for part in range(2):
                    block = [spread_rows(part, s, f, r, inside) for r in tiles]
                    line = jnp.concatenate(block, axis=0).astype(BF16)
                    size = 8 * len(block)
                    spread[part, f * size : (f + 1) * size, :] = line
            total = fields * 8 * len(tiles)
            out = jnp.dot(spread[0, :total], spreading, preferred_element_type=F32)
            out = out + jnp.dot(spread[1, :total], spreading, preferred_element_type=F32)
            out = out.reshape(fields, len(tiles), 8, LANES)
            for f in range(fields):
                for n, r in enumerate(tiles):
                    at = pl.ds(8 * r, 8)
                    block = out[f, n]
                    held[0, f, slot, at, :] = jnp.where(lane < 2, block, held[0, f, slot, at, :])
                    last = lane_tiles - 1
                    held[last, f, slot, at, :] = jnp.where(
                        lane >= LANES - 2, block, held[last, f, slot, at, :]
                    )

    def arrive(s):
        for k in range(lane_tiles):
            loads(s, k).wait()

    for h in halos:
        halo(*h).wait()
    arrive(-1)
    arrive(0)
    if merge:
        merge_shell(0, shells - 1, None)
        merge_shell(1, 0, True)

    def shell(s, last):
        if last:
            arrive(shells)
            if merge:
                merge_shell(shells + 1, 0, False)
        else:
            arrive(s + 1)
            if merge:
                merge_shell(s + 2, s + 1, True)
        inverse = inverse_ref[s]
        a_r = step * 0.5 / shell_step
        a_t = (step / (12.0 * theta_step)) * inverse
        c_r = step * spacing / (shell_step * shell_step)
        c_t = (step * spacing / (12.0 * theta_step * theta_step)) * (inverse * inverse)
        for n, k in enumerate(tiles_here):
            over = sine_ref[k : k + 1, :] * inverse
            a_p = jnp.broadcast_to((step / (12.0 * phi_step)) * over, (8, LANES))
            c_p = jnp.broadcast_to(
                (step * spacing / (12.0 * phi_step * phi_step)) * (over * over), (8, LANES)
            )
            for c in range(cols // 8):

                def load(f, ds, dc, dk):
                    if not 0 <= k + dk < lane_tiles:
                        return jnp.zeros((8, LANES), F32)
                    return held[k + dk, f, s + 1 + ds, FIRST + 8 * c + dc : FIRST + 8 * c + dc + 8, :]

                new = section_chunk(load, (a_r, a_t, a_p, c_r, c_t, c_p), lane)
                for f in range(fields):
                    made[n, s, f, 8 * c : 8 * c + 8, :] = new[f]
            store(s, n, k).start()

    @pl.loop(0, shells - 1)
    def _(s):
        shell(s, False)

    shell(shells - 1, True)
    for s in range(shells):
        for n, k in enumerate(tiles_here):
            store(s, n, k).wait()


def section_call(tiles_here, inverse, sine, x, faces, halos, borders=None, before=None):
    fields, shells, cols, rows = x.shape
    merge = borders is not None
    lane_tiles = rows // LANES
    vmem = pl.BlockSpec(memory_space=pltpu.VMEM)
    anywhere = pl.BlockSpec(memory_space=pl.ANY)
    operands = [inverse, sine, x, *faces, *halos]
    specs = [pl.BlockSpec(memory_space=pltpu.SMEM), vmem] + [anywhere] * 5
    scratch = [
        pltpu.VMEM((lane_tiles, fields, shells + 2, ROWS, LANES), F32),
        pltpu.VMEM((len(tiles_here), shells, fields, cols, LANES), F32),
    ]
    aliases = {}
    if merge:
        operands += [*borders, before]
        specs += [vmem] * 5 + [anywhere]
        aliases = {len(operands) - 1: 0}
        scratch += [
            pltpu.VMEM((5, 2, fields * shells, LANES), F32),
            pltpu.VMEM((2, fields * ROWS, LANES), BF16),
        ]
    scratch += [
        pltpu.SemaphoreType.DMA((shells + 2, lane_tiles)),
        pltpu.SemaphoreType.DMA((2, 2, lane_tiles)),
        pltpu.SemaphoreType.DMA((len(tiles_here), shells)),
    ]
    phi_count = cols * lax.axis_size("tile")
    return pl.pallas_call(
        functools.partial(
            section_kernel, tuple(tiles_here), merge, shells, cols, rows, phi_count
        ),
        out_shape=jax.ShapeDtypeStruct(x.shape, F32),
        in_specs=specs,
        out_specs=anywhere,
        scratch_shapes=scratch,
        input_output_aliases=aliases,
        compiler_params=pltpu.CompilerParams(vmem_limit_bytes=40 * 2**20),
        cost_estimate=pl.CostEstimate(
            flops=2 * 10**8, bytes_accessed=8 * 2**20, transcendentals=10**5
        ),
        name="border_tiles" if merge else "inner_tiles",
    )(*operands)


def shifted(x, axis, by):
    peers = lax.axis_size(axis)
    route = [(i, i + by) for i in range(peers) if 0 <= i + by < peers]
    return lax.ppermute(x, axis, route)


def on_device(state, donor_base, fractions, dest_pos):
    x = state[0]
    fields, shells, cols, rows = x.shape
    tiles = lax.axis_size("tile")
    theta_step, phi_step, shell_step, spacing = geometry(rows, cols * tiles)
    panel = lax.axis_index("panel").astype(jnp.int32).reshape(1)

    below = shifted(x[:, shells - 1], "rad", 1)
    above = shifted(x[:, 0], "rad", -1)

    payload, edge_cols = payload_call(
        panel, x.reshape(fields * shells, cols, rows), donor_base[0, 0], fractions[0, 0]
    )
    edge_cols = edge_cols.reshape(4, fields, shells, rows)
    before = shifted(edge_cols[2:], "tile", 1)
    after = shifted(edge_cols[:2], "tile", -1)

    got = lax.all_to_all(payload, ("panel", "tile"), split_axis=0, concat_axis=0, tiled=True)

    colat = 0.25 * math.pi + (np.arange(rows) + 0.5) * theta_step
    sine = jnp.asarray((1.0 / np.sin(colat)).reshape(-1, LANES), F32)
    layers = lax.axis_size("rad") * shells
    radius = BASE_RADIUS + (np.arange(layers) + 0.5) * shell_step
    inverse = lax.dynamic_slice_in_dim(
        jnp.asarray(1.0 / radius, F32), lax.axis_index("rad") * shells, shells
    )
    lane_tiles = rows // LANES
    inner = tuple(range(1, lane_tiles - 1))
    outer = (0, lane_tiles - 1)
    faces, halos = (below, above), (before, after)
    first = section_call(inner, inverse, sine, x, faces, halos)

    border = place_call(panel, got, dest_pos[0, 0])
    borders = (
        border,
        shifted(border, "rad", 1),
        shifted(border, "rad", -1),
        shifted(border, "tile", 1),
        shifted(border, "tile", -1),
    )
    updated = section_call(outer, inverse, sine, x, faces, halos, borders, first)
    return updated[None]


def solution(mesh):
    placed = (
        P("panel", None, "rad", "tile", None),
        P("panel", "tile", None, None),
        P("panel", "tile", None, None, None),
        P("panel", "tile", None, None),
    )
    return jax.shard_map(
        on_device,
        mesh=mesh,
        in_specs=placed,
        out_specs=P("panel", None, "rad", "tile", None),
        check_vma=False,
    )
```

```python
import functools
import math

import jax
import jax.numpy as jnp
import numpy as np
from jax import lax
from jax.experimental import pallas as pl
from jax.experimental.pallas import tpu as pltpu
from jax.sharding import PartitionSpec as P

BASE_RADIUS = 0.6
F32 = jnp.float32
BF16 = jnp.bfloat16
LANES = 128
FIRST = 8
ROWS = 48
PAYLOAD_VMEM = 60 * 2**20
SECTION_VMEM = 50 * 2**20
GATHER_VMEM = 50 * 2**20
SECTION_WEIGHT = 2 * 10**13
AHEAD = 4


def geometry(theta_count, phi_count):
    theta_step = 0.5 * math.pi / theta_count
    phi_step = 1.5 * math.pi / phi_count
    shell_step = 0.6 * min(theta_step, phi_step)
    corner = BASE_RADIUS * math.sin(0.25 * math.pi)
    spacing = min(shell_step, corner * theta_step, corner * phi_step)
    return (theta_step, phi_step, shell_step, spacing)


def halves(x):
    high = x.astype(BF16)
    return high, (x - high.astype(F32)).astype(BF16)


def lane_order(table):
    return jnp.concatenate([table[s : s + 1, :] for s in range(table.shape[0])], axis=1)


def turn(x):
    return jnp.transpose(jnp.concatenate([x] * (LANES // x.shape[0]), axis=0))


def stencils(base, fractions, cols, rows):
    base = lane_order(base)
    frac_theta = lane_order(fractions[0])
    frac_phi = lane_order(fractions[1])
    phi = base // rows
    theta = base - phi * rows
    position = lax.broadcasted_iota(jnp.int32, (rows, LANES), 0)
    along_theta = jnp.where(position == theta, 1.0 - frac_theta, 0.0)
    along_theta = along_theta + jnp.where(position == theta + 1, frac_theta, 0.0)
    place = lax.broadcasted_iota(jnp.int32, (cols, LANES), 0)
    along_phi = jnp.where(place == phi, 1.0 - frac_phi, 0.0)
    along_phi = along_phi + jnp.where(place == phi + 1, frac_phi, 0.0)
    return jnp.concatenate(halves(along_theta), axis=1), along_phi


def overset(block, both, along_phi):
    cols = along_phi.shape[0]
    x_high, x_low = halves(block)
    wide = jnp.dot(x_high, both, preferred_element_type=F32)
    low = jnp.dot(x_low, both[:, :LANES], preferred_element_type=F32)
    line = (wide[:, :LANES] + wide[:, LANES:] + low).reshape(-1, cols, LANES)
    return jnp.sum(line * along_phi[None], axis=1)


def edges_kernel(
    x_ref, dest_ref, up_ref, down_ref, left_ref, right_ref, faces, edges, dest_in, *sems
):
    fields, shells, cols, rows = x_ref.shape
    lane_tiles = rows // LANES
    face_sem, edge_sem, dest_sem, out_sem = sems
    points = pltpu.make_async_copy(dest_ref, dest_in, dest_sem)
    points.start()
    ends = [
        pltpu.make_async_copy(
            x_ref.at[:, (shells - 1, 0)[side], :, pl.ds(k * LANES, LANES)],
            faces.at[side, pl.ds(k * fields, fields)],
            face_sem.at[side, k],
        )
        for side in range(2)
        for k in range(lane_tiles)
    ]
    sides = [
        pltpu.make_async_copy(
            x_ref.at[:, :, (0, cols - 2)[side] + c, :],
            edges.at[side, c, pl.ds(0, fields)],
            edge_sem.at[side, c],
        )
        for side in range(2)
        for c in range(2)
    ]
    stores = [
        pltpu.make_async_copy(source, ref, out_sem.at[n])
        for n, (source, ref) in enumerate(
            (
                (faces.at[0], up_ref),
                (faces.at[1], down_ref),
                (edges.at[0], left_ref),
                (edges.at[1], right_ref),
            )
        )
    ]
    for copy in ends + sides:
        copy.start()
    points.wait()
    table = jnp.broadcast_to(lane_order(dest_in[...].astype(F32)), (shells, LANES))
    for side in range(2):
        edges[side, 0, fields, :, :LANES] = table
    for n in range(2):
        for copy in ends[n * lane_tiles : (n + 1) * lane_tiles]:
            copy.wait()
        stores[n].start()
    for n in range(2):
        for copy in sides[2 * n : 2 * n + 2]:
            copy.wait()
        stores[2 + n].start()
    for copy in stores:
        copy.wait()


def edges_call(x, dest):
    fields, shells, cols, rows = x.shape
    lane_tiles = rows // LANES
    anywhere = pl.BlockSpec(memory_space=pl.ANY)
    face = jax.ShapeDtypeStruct((lane_tiles * fields, cols, LANES), F32)
    edge = jax.ShapeDtypeStruct((2, fields + 1, shells, rows), F32)
    return pl.pallas_call(
        edges_kernel,
        out_shape=(face, face, edge, edge),
        in_specs=[anywhere] * 2,
        out_specs=(anywhere,) * 4,
        scratch_shapes=[
            pltpu.VMEM((2, *face.shape), F32),
            pltpu.VMEM((2, *edge.shape), F32),
            pltpu.VMEM(dest.shape, dest.dtype),
            pltpu.SemaphoreType.DMA((2, lane_tiles)),
            pltpu.SemaphoreType.DMA((2, 2)),
            pltpu.SemaphoreType.DMA,
            pltpu.SemaphoreType.DMA((4,)),
        ],
        compiler_params=pltpu.CompilerParams(vmem_limit_bytes=PAYLOAD_VMEM),
        cost_estimate=pl.CostEstimate(flops=10**6, bytes_accessed=2**21, transcendentals=0),
        name="edges",
    )(x, dest)


def payload_kernel(
    x_ref, base_ref, frac_ref, values_ref, held, values, base_in, frac_in, load_sem, small_sem
):
    fields, shells, cols, rows = held.shape
    smalls = [
        pltpu.make_async_copy(ref, target, small_sem.at[n])
        for n, (ref, target) in enumerate(((base_ref, base_in), (frac_ref, frac_in)))
    ]

    def load(f):
        return pltpu.make_async_copy(x_ref.at[f], held.at[f], load_sem.at[f])

    for copy in smalls:
        copy.start()
    for f in range(AHEAD):
        load(f).start()
    for copy in smalls:
        copy.wait()
    both, along_phi = stencils(base_in[...], frac_in[...], cols, rows)
    for f in range(fields):
        load(f).wait()
        if f + AHEAD < fields:
            load(f + AHEAD).start()
        block = held[f].reshape(shells * cols, rows)
        values[f * shells : (f + 1) * shells, :] = overset(block, both, along_phi)
    last = pltpu.make_async_copy(values, values_ref, small_sem.at[0])
    last.start()
    last.wait()


def payload_call(x, base, fractions):
    fields, shells, cols, rows = x.shape
    anywhere = pl.BlockSpec(memory_space=pl.ANY)
    points = jax.ShapeDtypeStruct((fields * shells, LANES), F32)
    return pl.pallas_call(
        payload_kernel,
        out_shape=points,
        in_specs=[anywhere] * 3,
        out_specs=anywhere,
        scratch_shapes=[
            pltpu.VMEM(x.shape, F32),
            pltpu.VMEM(points.shape, F32),
            pltpu.VMEM(base.shape, base.dtype),
            pltpu.VMEM(fractions.shape, F32),
            pltpu.SemaphoreType.DMA((fields,)),
            pltpu.SemaphoreType.DMA((2,)),
        ],
        compiler_params=pltpu.CompilerParams(vmem_limit_bytes=PAYLOAD_VMEM),
        cost_estimate=pl.CostEstimate(flops=10**9, bytes_accessed=6 * 2**20, transcendentals=0),
        name="payload",
    )(x, base, fractions)


def gather_kernel(
    values_ref, base_ref, frac_ref, below_ref, above_ref, out_ref, values, base, frac, faces, sem
):
    cols = faces.shape[2]
    lane_tiles = faces.shape[1] // 8
    sources = (values_ref, base_ref, frac_ref, below_ref, above_ref)
    targets = (values, base, frac, faces.at[0], faces.at[1])
    copies = [
        pltpu.make_async_copy(source, target, sem.at[n])
        for n, (source, target) in enumerate(zip(sources, targets))
    ]
    for copy in copies:
        copy.start()
    out_ref[...] = jnp.zeros(out_ref.shape, F32)
    tiles = out_ref.shape[0] // 16
    start = pl.multiple_of((1 - lax.axis_index("panel")) * (8 * tiles), 8 * tiles)
    for copy in copies[:3]:
        copy.wait()
    both, along_phi = stencils(base[...], frac[...], cols, lane_tiles * LANES)
    value = values[...]
    turned = turn(jnp.concatenate([value, pltpu.roll(value, 64, axis=1)], axis=0))
    row = lax.broadcasted_iota(jnp.int32, (tiles, LANES), 0)
    for n in range(2):
        own = turned[n * tiles : (n + 1) * tiles]
        before = jnp.where(row == 0, 0.0, pltpu.roll(own, 1, axis=0))
        after = jnp.where(row == tiles - 1, 0.0, pltpu.roll(own, tiles - 1, axis=0))
        for k, part in enumerate((own, before, after)):
            out_ref[pl.ds(start + (2 * k + n), tiles, stride=8), :] = part
    ends = []
    for side in range(2):
        copies[3 + side].wait()
        block = [
            faces[side, 8 * k : 8 * k + 8].reshape(8 * cols, LANES) for k in range(lane_tiles)
        ]
        ends.append(overset(jnp.concatenate(block, axis=1), both, along_phi))
    value = jnp.concatenate(ends, axis=0)
    parts = [value] + [pltpu.roll(value, LANES - tiles * s, axis=1) for s in range(1, 4)]
    turned = turn(jnp.concatenate(parts, axis=0))
    out_ref[pl.ds(start + 6, tiles, stride=8), :] = turned[:tiles]


def gather_call(values, base, fractions, below, above, tiles):
    vmem = pl.BlockSpec(memory_space=pltpu.VMEM)
    anywhere = pl.BlockSpec(memory_space=pl.ANY)
    return pl.pallas_call(
        gather_kernel,
        out_shape=jax.ShapeDtypeStruct((16 * tiles, LANES), F32),
        in_specs=[anywhere] * 5,
        out_specs=vmem,
        scratch_shapes=[
            pltpu.VMEM(values.shape, F32),
            pltpu.VMEM(base.shape, base.dtype),
            pltpu.VMEM(fractions.shape, F32),
            pltpu.VMEM((2, *below.shape), F32),
            pltpu.SemaphoreType.DMA((5,)),
        ],
        compiler_params=pltpu.CompilerParams(vmem_limit_bytes=GATHER_VMEM),
        cost_estimate=pl.CostEstimate(flops=10**6, bytes_accessed=2**18, transcendentals=0),
        name="gather",
    )(values, base, fractions, below, above)


def placed_points(got_ref, dest_ref, edge, split):
    tiles = got_ref.shape[0] // 8
    lane = lax.broadcasted_iota(jnp.int32, (64, LANES), 1)

    def rows(k):
        return got_ref[pl.ds(k, tiles, stride=8), :]

    def put(n, values, points):
        placing = jnp.where(
            lax.broadcasted_iota(jnp.int32, (LANES, LANES), 0) == points.astype(jnp.int32), 1.0, 0.0
        ).astype(BF16)
        dims = (((1,), (1,)), ((), ()))
        high, low = halves(values)
        count = values.shape[0]
        for part, value in enumerate((high, low)):
            split[n, part, :count, :] = lax.dot_general(
                value, placing, dims, preferred_element_type=F32
            )

    def tile_points(k):
        turned = turn(jnp.concatenate([rows(k), rows(k + 1)], axis=0))
        return jnp.where(lane < 64, turned[:64], turned[64:])

    own = lane_order(dest_ref[...].astype(F32))
    put(0, tile_points(0), own)
    turned = turn(rows(6))
    faces = turned[:16]
    for s in range(1, 4):
        faces = jnp.where(lane[:16] // tiles == s, turned[16 * s : 16 * s + 16], faces)
    put(1, faces, own)
    put(2, tile_points(2), edge[0])
    put(3, tile_points(4), edge[1])


def section_chunk(load, scale, lane):
    a_r, a_t, a_p, c_r, c_t, c_p = scale
    c_mid = 2.0 * c_r + 30.0 * c_t + 30.0 * c_p

    def parts(f, laplace=True):
        x = load(f, 0, 0, 0)
        left, right = load(f, 0, 0, -1), load(f, 0, 0, 1)
        inner, outer = load(f, -1, 0, 0), load(f, 1, 0, 0)
        t1 = pltpu.roll(jnp.where(lane < 1, right, x), LANES - 1, axis=1)
        t2 = pltpu.roll(jnp.where(lane < 2, right, x), LANES - 2, axis=1)
        s1 = pltpu.roll(jnp.where(lane >= LANES - 1, left, x), 1, axis=1)
        s2 = pltpu.roll(jnp.where(lane >= LANES - 2, left, x), 2, axis=1)
        p1, p2 = load(f, 0, 1, 0), load(f, 0, 2, 0)
        q1, q2 = load(f, 0, -1, 0), load(f, 0, -2, 0)
        g_r = outer - inner
        g_t = 8.0 * (t1 - s1) - (t2 - s2)
        g_p = 8.0 * (p1 - q1) - (p2 - q2)
        if not laplace:
            return x, g_r, g_t, g_p, None
        lap = c_r * (outer + inner) + c_t * (16.0 * (t1 + s1) - (t2 + s2))
        lap = lap + c_p * (16.0 * (p1 + q1) - (p2 + q2)) - c_mid * x
        return x, g_r, g_t, g_p, lap

    vel = tuple(load(1 + i, 0, 0, 0) * a for i, a in enumerate((a_r, a_t, a_p)))
    mag = tuple(load(4 + i, 0, 0, 0) * a for i, a in enumerate((a_r, a_t, a_p)))

    def along(v, g):
        return v[0] * g[0] + v[1] * g[1] + v[2] * g[2]

    new = [None] * 8
    rho, *g_rho, _ = parts(0, laplace=False)
    inv_rho = jnp.exp(-rho)
    rho_adv = along(vel, g_rho)
    pres, *g_pres, lap = parts(7)
    part_pres = pres - along(vel, g_pres) + 0.3 * lap
    div = None
    part_mag = []
    for i, a in enumerate((a_r, a_t, a_p)):
        u, *g_u, lap_u = parts(1 + i)
        b, *g_b, lap_b = parts(4 + i)
        term = a * g_u[i]
        div = term if div is None else div + term
        force = along(mag, g_b) - a * g_pres[i]
        new[1 + i] = u - along(vel, g_u) + inv_rho * force + 0.25 * lap_u
        part_mag.append((b, b - along(vel, g_b) + along(mag, g_u) + 0.2 * lap_b))
    for i, (b, part) in enumerate(part_mag):
        new[4 + i] = part - b * div
    new[0] = rho - rho_adv - div
    new[7] = part_pres - (5.0 / 3.0) * pres * div
    return new


def section_kernel(tiles_here, merge, cols, rows, phi_count, *refs):
    tables_ref, x_ref, before_ref, after_ref, below_ref, above_ref, *refs = refs
    fields, shells = x_ref.shape[:2]
    if merge:
        got_ref, dest_ref, _, *refs = refs
    out_ref, held, made, sides, tables, in_sem, halo_sem, small_sem, out_sem, *refs = refs
    if merge:
        got, dest, split, spread = refs
    lane_tiles = rows // LANES
    theta_step, phi_step, shell_step, spacing = geometry(rows, phi_count)
    step = 0.2 * spacing

    def loads(s):
        if isinstance(s, int) and s in (-1, shells):
            faces = below_ref if s == -1 else above_ref
            return [
                pltpu.make_async_copy(
                    faces.at[pl.ds(k * fields, fields)],
                    held.at[k, :, pl.ds((s + 1) * ROWS + FIRST, cols), :],
                    in_sem.at[s + 1, k],
                )
                for k in tiles_here
            ]
        return [
            pltpu.make_async_copy(
                x_ref.at[:, s, :, pl.ds(k * LANES, LANES)],
                held.at[k, :, pl.ds((s + 1) * ROWS + FIRST, cols), :],
                in_sem.at[s + 1, k],
            )
            for k in range(lane_tiles)
        ]

    def halo(side):
        ref = (before_ref, after_ref)[side]
        return pltpu.make_async_copy(ref, sides.at[side], halo_sem.at[side])

    def store(s, k):
        return pltpu.make_async_copy(
            made.at[k, s], out_ref.at[:, s, :, pl.ds(k * LANES, LANES)], out_sem.at[k, s]
        )

    slab = tables_ref.at[lax.axis_index("rad")]
    smalls = [pltpu.make_async_copy(slab, tables, small_sem.at[0])]
    if merge:
        start = pl.multiple_of((1 - lax.axis_index("panel")) * got.shape[0], got.shape[0])
        smalls.append(
            pltpu.make_async_copy(
                got_ref.at[pl.ds(start, got.shape[0])], got, small_sem.at[1]
            )
        )
        smalls.append(pltpu.make_async_copy(dest_ref, dest, small_sem.at[2]))
    for copy in smalls:
        copy.start()
    for side in range(2):
        halo(side).start()
    for copy in loads(-1) + loads(shells):
        copy.start()
    for s in range(AHEAD):
        for copy in loads(s):
            copy.start()
    for copy in smalls:
        copy.wait()

    lane = lax.broadcasted_iota(jnp.int32, (8, LANES), 1)

    for side in range(2):
        halo(side).wait()
    for side in range(2):
        for c in range(2):
            at = ROWS + (FIRST - 2, FIRST + cols)[side] + c
            for k in tiles_here:
                for f in range(fields):
                    held[k, f, pl.ds(at, shells, stride=ROWS), :] = sides[
                        side, c, f, :, k * LANES : (k + 1) * LANES
                    ]

    if merge:
        edge = [sides[side, 0, fields, 0:1, :LANES] for side in range(2)]
        placed_points(got, dest, edge, split)
        wide = lax.broadcasted_iota(jnp.int32, (LANES, LANES), 1)
        group = lax.broadcasted_iota(jnp.int32, (LANES, LANES), 0) // cols
        target = jnp.where(group < 2, group, LANES - 4 + group)
        spreading = jnp.where(wide == target, 1.0, 0.0).astype(BF16)
        row = lax.broadcasted_iota(jnp.int32, (8, LANES), 0)
        within = lane % cols

        def spread_rows(part, s, f, r):
            if isinstance(s, int) and s in (-1, shells):
                index = f if s == -1 else fields + f
                wanted, which = within == row + (8 * r - FIRST), 1
            else:
                index = f * shells + s
                if r == 0:
                    wanted, which = (row >= 6) & (within == row + (cols - 8)), 2
                elif r == ROWS // 8 - 1:
                    wanted, which = (row < 2) & (within == row), 3
                else:
                    wanted, which = within == row + (8 * r - FIRST), 0
            return jnp.where(wanted, split[which, part, pl.ds(index, 1), :], 0.0)

        def merge_shell(s):
            inside = not isinstance(s, int) or 0 <= s < shells
            tiles = range(ROWS // 8) if inside else range(1, ROWS // 8 - 1)
            for f in range(fields):
                for part in range(2):
                    block = [spread_rows(part, s, f, r) for r in tiles]
                    line = jnp.concatenate(block, axis=0).astype(BF16)
                    size = 8 * len(block)
                    spread[part, f * size : (f + 1) * size, :] = line
            total = fields * 8 * len(tiles)
            out = jnp.dot(spread[0, :total], spreading, preferred_element_type=F32)
            out = out + jnp.dot(spread[1, :total], spreading, preferred_element_type=F32)
            out = out.reshape(fields, len(tiles), 8, LANES)
            last = lane_tiles - 1
            for f in range(fields):
                for n, r in enumerate(tiles):
                    at = (f, pl.ds(pl.multiple_of((s + 1) * ROWS + 8 * r, 8), 8), slice(None))
                    block = out[f, n]
                    held[(0, *at)] = jnp.where(lane < 2, block, held[(0, *at)])
                    held[(last, *at)] = jnp.where(lane >= LANES - 2, block, held[(last, *at)])

    def compute(s, k):
        inverse = tables[pl.ds(8 + s, 1), :]
        over = tables[k : k + 1, :] * inverse

        def wide(row):
            return jnp.broadcast_to(row, (8, LANES))

        a_r = step * 0.5 / shell_step
        a_t = wide((step / (12.0 * theta_step)) * inverse)
        a_p = wide((step / (12.0 * phi_step)) * over)
        c_r = step * spacing / (shell_step * shell_step)
        c_t = wide((step * spacing / (12.0 * theta_step * theta_step)) * (inverse * inverse))
        c_p = wide((step * spacing / (12.0 * phi_step * phi_step)) * (over * over))

        for c in range(cols // 8):

            def load(f, ds, dc, dk):
                if not 0 <= k + dk < lane_tiles:
                    return jnp.zeros((8, LANES), F32)
                at = pl.multiple_of((s + 1 + ds) * ROWS + FIRST + 8 * c, 8)
                return held[k + dk, f, pl.ds(at + dc, 8), :]

            new = section_chunk(load, (a_r, a_t, a_p, c_r, c_t, c_p), lane)
            for f in range(fields):
                made[k, s, f, 8 * c : 8 * c + 8, :] = new[f]

        store(s, k).start()

    for s in (-1, shells):
        for copy in loads(s):
            copy.wait()
        if merge:
            merge_shell(s)

    @pl.loop(0, shells + 1)
    def _(t):
        @pl.when(t < shells)
        def _():
            @pl.when(t + AHEAD < shells)
            def _():
                for copy in loads(t + AHEAD):
                    copy.start()

            for copy in loads(t):
                copy.wait()
            if merge:
                merge_shell(t)

        @pl.when(t > 0)
        def _():
            for k in tiles_here:
                compute(t - 1, k)

    for s in range(shells):
        for k in tiles_here:
            store(s, k).wait()


def section_call(name, tiles_here, tables, x, halos, faces, found=(), before=None):
    fields, shells, cols, rows = x.shape
    lane_tiles = rows // LANES
    merge = before is not None
    anywhere = pl.BlockSpec(memory_space=pl.ANY)
    operands = [tables, x, *halos, *faces, *found]
    scratch = [
        pltpu.VMEM((lane_tiles, fields, (shells + 2) * ROWS, LANES), F32),
        pltpu.VMEM((lane_tiles, shells, fields, cols, LANES), F32),
        pltpu.VMEM((2, *halos[0].shape), F32),
        pltpu.VMEM(tables.shape[1:], F32),
        pltpu.SemaphoreType.DMA((shells + 2, lane_tiles)),
        pltpu.SemaphoreType.DMA((2,)),
        pltpu.SemaphoreType.DMA((3,)),
        pltpu.SemaphoreType.DMA((lane_tiles, shells)),
    ]
    aliases = {}
    if merge:
        aliases = {len(operands): 0}
        operands.append(before)
        got, dest = found
        scratch += [
            pltpu.VMEM((got.shape[0] // 2, LANES), F32),
            pltpu.VMEM(dest.shape, dest.dtype),
            pltpu.VMEM((4, 2, fields * shells, LANES), F32),
            pltpu.VMEM((2, fields * ROWS, LANES), BF16),
        ]
    phi_count = cols * lax.axis_size("tile")
    return pl.pallas_call(
        functools.partial(section_kernel, tiles_here, merge, cols, rows, phi_count),
        out_shape=jax.ShapeDtypeStruct(x.shape, F32),
        in_specs=[anywhere] * len(operands),
        out_specs=anywhere,
        scratch_shapes=scratch,
        input_output_aliases=aliases,
        compiler_params=pltpu.CompilerParams(vmem_limit_bytes=SECTION_VMEM),
        cost_estimate=pl.CostEstimate(
            flops=SECTION_WEIGHT, bytes_accessed=8 * 2**20, transcendentals=2**17
        ),
        name=name,
    )(*operands)


def shifted(x, axis, by):
    peers = lax.axis_size(axis)
    route = [(i, i + by) for i in range(peers) if 0 <= i + by < peers]
    return lax.ppermute(x, axis, route)


def on_device(state, donor_base, fractions, dest_pos):
    x = state[0]
    fields, shells, cols, rows = x.shape
    tiles = lax.axis_size("tile")
    theta_step, phi_step, shell_step, spacing = geometry(rows, cols * tiles)
    dest = dest_pos[0, 0].T

    base, parts = donor_base[0, 0].T, jnp.swapaxes(fractions[0, 0], 1, 2)
    up, down, left, right = edges_call(x, dest)
    faces = (shifted(up, "rad", 1), shifted(down, "rad", -1))
    halos = (shifted(right, "tile", 1), shifted(left, "tile", -1))
    values = payload_call(x, base, parts)
    sent = gather_call(values, base, parts, *faces, tiles)

    colat = 0.25 * math.pi + (np.arange(rows) + 0.5) * theta_step
    peers = lax.axis_size("rad")
    radius = BASE_RADIUS + (np.arange(peers * shells) + 0.5) * shell_step
    every = np.zeros((peers, 8 + shells, LANES), np.float32)
    every[:, : rows // LANES] = (1.0 / np.sin(colat)).reshape(1, -1, LANES)
    every[:, 8:] = (1.0 / radius).reshape(peers, shells, 1)
    tables = jnp.asarray(every)
    last = rows // LANES - 1

    got = lax.all_to_all(sent, ("panel", "tile"), split_axis=0, concat_axis=0, tiled=True)
    new = section_call("inner", tuple(range(1, last)), tables, x, halos, faces)
    new = section_call("outer", (0, last), tables, x, halos, faces, (got, dest), new)
    return new[None]


def solution(mesh):
    placed = (
        P("panel", None, "rad", "tile", None),
        P("panel", "tile", None, None),
        P("panel", "tile", None, None, None),
        P("panel", "tile", None, None),
    )
    return jax.shard_map(
        on_device,
        mesh=mesh,
        in_specs=placed,
        out_specs=P("panel", None, "rad", "tile", None),
        check_vma=False,
    )
```

```python
import functools
import math

import jax
import jax.numpy as jnp
import numpy as np
from jax import lax
from jax.experimental import pallas as pl
from jax.experimental.pallas import tpu as pltpu
from jax.sharding import PartitionSpec as P

BASE_RADIUS = 0.6
F32 = jnp.float32
BF16 = jnp.bfloat16
LANES = 128
FIRST = 8
ROWS = 48
EDGES_VMEM = 60 * 2**20
PAYLOAD_VMEM = 50 * 2**20
SECTION_VMEM = 50 * 2**20
GATHER_VMEM = 50 * 2**20
SECTION_WEIGHT = 2 * 10**13
AHEAD = 4


def geometry(theta_count, phi_count):
    theta_step = 0.5 * math.pi / theta_count
    phi_step = 1.5 * math.pi / phi_count
    shell_step = 0.6 * min(theta_step, phi_step)
    corner = BASE_RADIUS * math.sin(0.25 * math.pi)
    spacing = min(shell_step, corner * theta_step, corner * phi_step)
    return (theta_step, phi_step, shell_step, spacing)


def halves(x):
    high = x.astype(BF16)
    return high, (x - high.astype(F32)).astype(BF16)


def lane_order(table):
    return jnp.concatenate([table[s : s + 1, :] for s in range(table.shape[0])], axis=1)


def turn(x):
    return jnp.transpose(jnp.concatenate([x] * (LANES // x.shape[0]), axis=0))


def stencils(base, fractions, cols, rows):
    base = lane_order(base)
    frac_theta = lane_order(fractions[0])
    frac_phi = lane_order(fractions[1])
    phi = base // rows
    theta = base - phi * rows
    position = lax.broadcasted_iota(jnp.int32, (rows, LANES), 0)
    along_theta = jnp.where(position == theta, 1.0 - frac_theta, 0.0)
    along_theta = along_theta + jnp.where(position == theta + 1, frac_theta, 0.0)
    place = lax.broadcasted_iota(jnp.int32, (cols, LANES), 0)
    along_phi = jnp.where(place == phi, 1.0 - frac_phi, 0.0)
    along_phi = along_phi + jnp.where(place == phi + 1, frac_phi, 0.0)
    return jnp.concatenate(halves(along_theta), axis=1), along_phi


def overset(block, both, along_phi):
    cols = along_phi.shape[0]
    x_high, x_low = halves(block)
    wide = jnp.dot(x_high, both, preferred_element_type=F32)
    low = jnp.dot(x_low, both[:, :LANES], preferred_element_type=F32)
    line = (wide[:, :LANES] + wide[:, LANES:] + low).reshape(-1, cols, LANES)
    return jnp.sum(line * along_phi[None], axis=1)


def edges_kernel(
    x_ref, dest_ref, near_face, far_face, near_edge, far_edge, faces, edges, dest_in, *sems
):
    fields, shells, cols, rows = x_ref.shape
    lane_tiles = rows // LANES
    face_sem, edge_sem, dest_sem, out_sem = sems
    points = pltpu.make_async_copy(dest_ref, dest_in, dest_sem)
    points.start()
    ends = [
        pltpu.make_async_copy(
            x_ref.at[:, (shells - 1, 0)[side], :, pl.ds(k * LANES, LANES)],
            faces.at[side, pl.ds(k * fields, fields)],
            face_sem.at[side, k],
        )
        for side in range(2)
        for k in range(lane_tiles)
    ]
    sides = [
        pltpu.make_async_copy(
            x_ref.at[:, :, (0, cols - 2)[side] + c, :],
            edges.at[side, c, pl.ds(0, fields)],
            edge_sem.at[side, c],
        )
        for side in range(2)
        for c in range(2)
    ]
    upper = lax.rem(lax.axis_index("rad"), 2)
    second = lax.rem(lax.axis_index("tile"), 2)
    stores = [
        pltpu.make_async_copy(source, ref, out_sem.at[n])
        for n, (source, ref) in enumerate(
            (
                (faces.at[upper], near_face),
                (faces.at[1 - upper], far_face),
                (edges.at[1 - second], near_edge),
                (edges.at[second], far_edge),
            )
        )
    ]
    for copy in ends + sides:
        copy.start()
    points.wait()
    table = jnp.broadcast_to(lane_order(dest_in[...].astype(F32)), (shells, LANES))
    for side in range(2):
        edges[side, 0, fields, :, :LANES] = table
    for copy in ends:
        copy.wait()
    for copy in stores[:2]:
        copy.start()
    for copy in sides:
        copy.wait()
    for copy in stores[2:]:
        copy.start()
    for copy in stores:
        copy.wait()


def edges_call(x, dest):
    fields, shells, cols, rows = x.shape
    lane_tiles = rows // LANES
    anywhere = pl.BlockSpec(memory_space=pl.ANY)
    face = jax.ShapeDtypeStruct((lane_tiles * fields, cols, LANES), F32)
    edge = jax.ShapeDtypeStruct((2, fields + 1, shells, rows), F32)
    return pl.pallas_call(
        edges_kernel,
        out_shape=(face, face, edge, edge),
        in_specs=[anywhere] * 2,
        out_specs=(anywhere,) * 4,
        scratch_shapes=[
            pltpu.VMEM((2, *face.shape), F32),
            pltpu.VMEM((2, *edge.shape), F32),
            pltpu.VMEM(dest.shape, dest.dtype),
            pltpu.SemaphoreType.DMA((2, lane_tiles)),
            pltpu.SemaphoreType.DMA((2, 2)),
            pltpu.SemaphoreType.DMA,
            pltpu.SemaphoreType.DMA((4,)),
        ],
        compiler_params=pltpu.CompilerParams(vmem_limit_bytes=EDGES_VMEM),
        cost_estimate=pl.CostEstimate(flops=10**6, bytes_accessed=2**21, transcendentals=0),
        name="edges",
    )(x, dest)


def payload_kernel(
    x_ref, base_ref, frac_ref, values_ref, held, values, base_in, frac_in, load_sem, small_sem
):
    fields, shells, cols, rows = held.shape
    smalls = [
        pltpu.make_async_copy(ref, target, small_sem.at[n])
        for n, (ref, target) in enumerate(((base_ref, base_in), (frac_ref, frac_in)))
    ]

    def load(f):
        return pltpu.make_async_copy(x_ref.at[f], held.at[f], load_sem.at[f])

    for copy in smalls:
        copy.start()
    for f in range(AHEAD):
        load(f).start()
    for copy in smalls:
        copy.wait()
    both, along_phi = stencils(base_in[...], frac_in[...], cols, rows)
    for f in range(fields):
        load(f).wait()
        if f + AHEAD < fields:
            load(f + AHEAD).start()
        block = held[f].reshape(shells * cols, rows)
        values[f * shells : (f + 1) * shells, :] = overset(block, both, along_phi)
    last = pltpu.make_async_copy(values, values_ref, small_sem.at[0])
    last.start()
    last.wait()


def payload_call(x, base, fractions):
    fields, shells, cols, rows = x.shape
    anywhere = pl.BlockSpec(memory_space=pl.ANY)
    points = jax.ShapeDtypeStruct((fields * shells, LANES), F32)
    return pl.pallas_call(
        payload_kernel,
        out_shape=points,
        in_specs=[anywhere] * 3,
        out_specs=anywhere,
        scratch_shapes=[
            pltpu.VMEM(x.shape, F32),
            pltpu.VMEM(points.shape, F32),
            pltpu.VMEM(base.shape, base.dtype),
            pltpu.VMEM(fractions.shape, F32),
            pltpu.SemaphoreType.DMA((fields,)),
            pltpu.SemaphoreType.DMA((2,)),
        ],
        compiler_params=pltpu.CompilerParams(vmem_limit_bytes=PAYLOAD_VMEM),
        cost_estimate=pl.CostEstimate(flops=10**9, bytes_accessed=6 * 2**20, transcendentals=0),
        name="payload",
    )(x, base, fractions)


def gather_kernel(
    values_ref, base_ref, frac_ref, near_ref, far_ref, out_ref, values, base, frac, faces, sem
):
    cols = faces.shape[2]
    lane_tiles = faces.shape[1] // 8
    upper = lax.rem(lax.axis_index("rad"), 2)
    sources = (values_ref, base_ref, frac_ref, near_ref, far_ref)
    targets = (values, base, frac, faces.at[1 - upper], faces.at[upper])
    copies = [
        pltpu.make_async_copy(source, target, sem.at[n])
        for n, (source, target) in enumerate(zip(sources, targets))
    ]
    for copy in copies:
        copy.start()
    out_ref[...] = jnp.zeros(out_ref.shape, F32)
    tiles = out_ref.shape[0] // 16
    start = pl.multiple_of((1 - lax.axis_index("panel")) * (8 * tiles), 8 * tiles)
    for copy in copies[:3]:
        copy.wait()
    both, along_phi = stencils(base[...], frac[...], cols, lane_tiles * LANES)
    value = values[...]
    turned = turn(jnp.concatenate([value, pltpu.roll(value, 64, axis=1)], axis=0))
    row = lax.broadcasted_iota(jnp.int32, (tiles, LANES), 0)
    for n in range(2):
        own = turned[n * tiles : (n + 1) * tiles]
        before = jnp.where(row == 0, 0.0, pltpu.roll(own, 1, axis=0))
        after = jnp.where(row == tiles - 1, 0.0, pltpu.roll(own, tiles - 1, axis=0))
        for k, part in enumerate((own, before, after)):
            out_ref[pl.ds(start + (2 * k + n), tiles, stride=8), :] = part
    ends = []
    for copy in copies[3:]:
        copy.wait()
    for side in range(2):
        block = [
            faces[side, 8 * k : 8 * k + 8].reshape(8 * cols, LANES) for k in range(lane_tiles)
        ]
        ends.append(overset(jnp.concatenate(block, axis=1), both, along_phi))
    value = jnp.concatenate(ends, axis=0)
    parts = [value] + [pltpu.roll(value, LANES - tiles * s, axis=1) for s in range(1, 4)]
    turned = turn(jnp.concatenate(parts, axis=0))
    out_ref[pl.ds(start + 6, tiles, stride=8), :] = turned[:tiles]


def gather_call(values, base, fractions, near, far, tiles):
    vmem = pl.BlockSpec(memory_space=pltpu.VMEM)
    anywhere = pl.BlockSpec(memory_space=pl.ANY)
    return pl.pallas_call(
        gather_kernel,
        out_shape=jax.ShapeDtypeStruct((16 * tiles, LANES), F32),
        in_specs=[anywhere] * 5,
        out_specs=vmem,
        scratch_shapes=[
            pltpu.VMEM(values.shape, F32),
            pltpu.VMEM(base.shape, base.dtype),
            pltpu.VMEM(fractions.shape, F32),
            pltpu.VMEM((2, *near.shape), F32),
            pltpu.SemaphoreType.DMA((5,)),
        ],
        compiler_params=pltpu.CompilerParams(vmem_limit_bytes=GATHER_VMEM),
        cost_estimate=pl.CostEstimate(flops=10**6, bytes_accessed=2**18, transcendentals=0),
        name="gather",
    )(values, base, fractions, near, far)


def placed_points(got_ref, dest_ref, edge, split):
    tiles = got_ref.shape[0] // 8
    lane = lax.broadcasted_iota(jnp.int32, (64, LANES), 1)

    def rows(k):
        return got_ref[pl.ds(k, tiles, stride=8), :]

    def put(n, values, points):
        placing = jnp.where(
            lax.broadcasted_iota(jnp.int32, (LANES, LANES), 0) == points.astype(jnp.int32), 1.0, 0.0
        ).astype(BF16)
        dims = (((1,), (1,)), ((), ()))
        high, low = halves(values)
        count = values.shape[0]
        for part, value in enumerate((high, low)):
            split[n, part, :count, :] = lax.dot_general(
                value, placing, dims, preferred_element_type=F32
            )

    def tile_points(k):
        turned = turn(jnp.concatenate([rows(k), rows(k + 1)], axis=0))
        return jnp.where(lane < 64, turned[:64], turned[64:])

    own = lane_order(dest_ref[...].astype(F32))
    put(0, tile_points(0), own)
    turned = turn(rows(6))
    faces = turned[:16]
    for s in range(1, 4):
        faces = jnp.where(lane[:16] // tiles == s, turned[16 * s : 16 * s + 16], faces)
    put(1, faces, own)
    put(2, tile_points(2), edge[0])
    put(3, tile_points(4), edge[1])


def section_chunk(load, scale, lane):
    a_r, a_t, a_p, c_r, c_t, c_p = scale
    c_mid = 2.0 * c_r + 30.0 * c_t + 30.0 * c_p

    def parts(f, laplace=True):
        x = load(f, 0, 0, 0)
        left, right = load(f, 0, 0, -1), load(f, 0, 0, 1)
        inner, outer = load(f, -1, 0, 0), load(f, 1, 0, 0)
        t1 = pltpu.roll(jnp.where(lane < 1, right, x), LANES - 1, axis=1)
        t2 = pltpu.roll(jnp.where(lane < 2, right, x), LANES - 2, axis=1)
        s1 = pltpu.roll(jnp.where(lane >= LANES - 1, left, x), 1, axis=1)
        s2 = pltpu.roll(jnp.where(lane >= LANES - 2, left, x), 2, axis=1)
        p1, p2 = load(f, 0, 1, 0), load(f, 0, 2, 0)
        q1, q2 = load(f, 0, -1, 0), load(f, 0, -2, 0)
        g_r = outer - inner
        g_t = 8.0 * (t1 - s1) - (t2 - s2)
        g_p = 8.0 * (p1 - q1) - (p2 - q2)
        if not laplace:
            return x, g_r, g_t, g_p, None
        lap = c_r * (outer + inner) + c_t * (16.0 * (t1 + s1) - (t2 + s2))
        lap = lap + c_p * (16.0 * (p1 + q1) - (p2 + q2)) - c_mid * x
        return x, g_r, g_t, g_p, lap

    vel = tuple(load(1 + i, 0, 0, 0) * a for i, a in enumerate((a_r, a_t, a_p)))
    mag = tuple(load(4 + i, 0, 0, 0) * a for i, a in enumerate((a_r, a_t, a_p)))

    def along(v, g):
        return v[0] * g[0] + v[1] * g[1] + v[2] * g[2]

    new = [None] * 8
    rho, *g_rho, _ = parts(0, laplace=False)
    inv_rho = jnp.exp(-rho)
    rho_adv = along(vel, g_rho)
    pres, *g_pres, lap = parts(7)
    part_pres = pres - along(vel, g_pres) + 0.3 * lap
    div = None
    part_mag = []
    for i, a in enumerate((a_r, a_t, a_p)):
        u, *g_u, lap_u = parts(1 + i)
        b, *g_b, lap_b = parts(4 + i)
        term = a * g_u[i]
        div = term if div is None else div + term
        force = along(mag, g_b) - a * g_pres[i]
        new[1 + i] = u - along(vel, g_u) + inv_rho * force + 0.25 * lap_u
        part_mag.append((b, b - along(vel, g_b) + along(mag, g_u) + 0.2 * lap_b))
    for i, (b, part) in enumerate(part_mag):
        new[4 + i] = part - b * div
    new[0] = rho - rho_adv - div
    new[7] = part_pres - (5.0 / 3.0) * pres * div
    return new


def section_kernel(tiles_here, merge, cols, rows, phi_count, *refs):
    tables_ref, x_ref, near_ref, far_ref, near_face, far_face, *refs = refs
    fields, shells = x_ref.shape[:2]
    if merge:
        got_ref, dest_ref, _, *refs = refs
    out_ref, held, made, sides, tables, in_sem, halo_sem, small_sem, out_sem, *refs = refs
    if merge:
        got, dest, split, spread = refs
    lane_tiles = rows // LANES
    theta_step, phi_step, shell_step, spacing = geometry(rows, phi_count)
    step = 0.2 * spacing

    upper = lax.rem(lax.axis_index("rad"), 2)
    second = lax.rem(lax.axis_index("tile"), 2)

    def face(n):
        ref, side = ((near_face, 1 - upper), (far_face, upper))[n]
        at = pl.multiple_of(side * (shells + 1) * ROWS + FIRST, 8)
        return [
            pltpu.make_async_copy(
                ref.at[pl.ds(k * fields, fields)],
                held.at[k, :, pl.ds(at, cols), :],
                in_sem.at[n * (shells + 1), k],
            )
            for k in tiles_here
        ]

    def loads(s):
        return [
            pltpu.make_async_copy(
                x_ref.at[:, s, :, pl.ds(k * LANES, LANES)],
                held.at[k, :, pl.ds((s + 1) * ROWS + FIRST, cols), :],
                in_sem.at[s + 1, k],
            )
            for k in range(lane_tiles)
        ]

    def halo(n):
        ref, side = ((near_ref, 1 - second), (far_ref, second))[n]
        return pltpu.make_async_copy(ref, sides.at[side], halo_sem.at[n])

    def store(s, k):
        return pltpu.make_async_copy(
            made.at[k, s], out_ref.at[:, s, :, pl.ds(k * LANES, LANES)], out_sem.at[k, s]
        )

    slab = tables_ref.at[lax.axis_index("rad")]
    smalls = [pltpu.make_async_copy(slab, tables, small_sem.at[0])]
    if merge:
        start = pl.multiple_of((1 - lax.axis_index("panel")) * got.shape[0], got.shape[0])
        smalls.append(
            pltpu.make_async_copy(
                got_ref.at[pl.ds(start, got.shape[0])], got, small_sem.at[1]
            )
        )
        smalls.append(pltpu.make_async_copy(dest_ref, dest, small_sem.at[2]))
    for copy in smalls:
        copy.start()
    for side in range(2):
        halo(side).start()
    for copy in face(0) + face(1):
        copy.start()
    for s in range(AHEAD):
        for copy in loads(s):
            copy.start()
    for copy in smalls:
        copy.wait()

    lane = lax.broadcasted_iota(jnp.int32, (8, LANES), 1)

    for side in range(2):
        halo(side).wait()
    for side in range(2):
        for c in range(2):
            at = ROWS + (FIRST - 2, FIRST + cols)[side] + c
            for k in tiles_here:
                for f in range(fields):
                    held[k, f, pl.ds(at, shells, stride=ROWS), :] = sides[
                        side, c, f, :, k * LANES : (k + 1) * LANES
                    ]

    if merge:
        edge = [sides[side, 0, fields, 0:1, :LANES] for side in range(2)]
        placed_points(got, dest, edge, split)
        wide = lax.broadcasted_iota(jnp.int32, (LANES, LANES), 1)
        group = lax.broadcasted_iota(jnp.int32, (LANES, LANES), 0) // cols
        target = jnp.where(group < 2, group, LANES - 4 + group)
        spreading = jnp.where(wide == target, 1.0, 0.0).astype(BF16)
        row = lax.broadcasted_iota(jnp.int32, (8, LANES), 0)
        within = lane % cols

        def spread_rows(part, s, f, r):
            if isinstance(s, int) and s in (-1, shells):
                index = f if s == -1 else fields + f
                wanted, which = within == row + (8 * r - FIRST), 1
            else:
                index = f * shells + s
                if r == 0:
                    wanted, which = (row >= 6) & (within == row + (cols - 8)), 2
                elif r == ROWS // 8 - 1:
                    wanted, which = (row < 2) & (within == row), 3
                else:
                    wanted, which = within == row + (8 * r - FIRST), 0
            return jnp.where(wanted, split[which, part, pl.ds(index, 1), :], 0.0)

        def merge_shell(s):
            inside = not isinstance(s, int) or 0 <= s < shells
            tiles = range(ROWS // 8) if inside else range(1, ROWS // 8 - 1)
            for f in range(fields):
                for part in range(2):
                    block = [spread_rows(part, s, f, r) for r in tiles]
                    line = jnp.concatenate(block, axis=0).astype(BF16)
                    size = 8 * len(block)
                    spread[part, f * size : (f + 1) * size, :] = line
            total = fields * 8 * len(tiles)
            out = jnp.dot(spread[0, :total], spreading, preferred_element_type=F32)
            out = out + jnp.dot(spread[1, :total], spreading, preferred_element_type=F32)
            out = out.reshape(fields, len(tiles), 8, LANES)
            last = lane_tiles - 1
            for f in range(fields):
                for n, r in enumerate(tiles):
                    at = (f, pl.ds(pl.multiple_of((s + 1) * ROWS + 8 * r, 8), 8), slice(None))
                    block = out[f, n]
                    held[(0, *at)] = jnp.where(lane < 2, block, held[(0, *at)])
                    held[(last, *at)] = jnp.where(lane >= LANES - 2, block, held[(last, *at)])

    def compute(s, k):
        inverse = tables[pl.ds(8 + s, 1), :]
        over = tables[k : k + 1, :] * inverse

        def wide(row):
            return jnp.broadcast_to(row, (8, LANES))

        a_r = step * 0.5 / shell_step
        a_t = wide((step / (12.0 * theta_step)) * inverse)
        a_p = wide((step / (12.0 * phi_step)) * over)
        c_r = step * spacing / (shell_step * shell_step)
        c_t = wide((step * spacing / (12.0 * theta_step * theta_step)) * (inverse * inverse))
        c_p = wide((step * spacing / (12.0 * phi_step * phi_step)) * (over * over))

        for c in range(cols // 8):

            def load(f, ds, dc, dk):
                if not 0 <= k + dk < lane_tiles:
                    return jnp.zeros((8, LANES), F32)
                at = pl.multiple_of((s + 1 + ds) * ROWS + FIRST + 8 * c, 8)
                return held[k + dk, f, pl.ds(at + dc, 8), :]

            new = section_chunk(load, (a_r, a_t, a_p, c_r, c_t, c_p), lane)
            for f in range(fields):
                made[k, s, f, 8 * c : 8 * c + 8, :] = new[f]

        store(s, k).start()

    for copy in face(0) + face(1):
        copy.wait()
    if merge:
        merge_shell(-1)
        merge_shell(shells)

    @pl.loop(0, shells + 1)
    def _(t):
        @pl.when(t < shells)
        def _():
            @pl.when(t + AHEAD < shells)
            def _():
                for copy in loads(t + AHEAD):
                    copy.start()

            for copy in loads(t):
                copy.wait()
            if merge:
                merge_shell(t)

        @pl.when(t > 0)
        def _():
            for k in tiles_here:
                compute(t - 1, k)

    for s in range(shells):
        for k in tiles_here:
            store(s, k).wait()


def section_call(name, tiles_here, tables, x, halos, faces, found=(), before=None):
    fields, shells, cols, rows = x.shape
    lane_tiles = rows // LANES
    merge = before is not None
    anywhere = pl.BlockSpec(memory_space=pl.ANY)
    operands = [tables, x, *halos, *faces, *found]
    scratch = [
        pltpu.VMEM((lane_tiles, fields, (shells + 2) * ROWS, LANES), F32),
        pltpu.VMEM((lane_tiles, shells, fields, cols, LANES), F32),
        pltpu.VMEM((2, *halos[0].shape), F32),
        pltpu.VMEM(tables.shape[1:], F32),
        pltpu.SemaphoreType.DMA((shells + 2, lane_tiles)),
        pltpu.SemaphoreType.DMA((2,)),
        pltpu.SemaphoreType.DMA((3,)),
        pltpu.SemaphoreType.DMA((lane_tiles, shells)),
    ]
    aliases = {}
    if merge:
        aliases = {len(operands): 0}
        operands.append(before)
        got, dest = found
        scratch += [
            pltpu.VMEM((got.shape[0] // 2, LANES), F32),
            pltpu.VMEM(dest.shape, dest.dtype),
            pltpu.VMEM((4, 2, fields * shells, LANES), F32),
            pltpu.VMEM((2, fields * ROWS, LANES), BF16),
        ]
    phi_count = cols * lax.axis_size("tile")
    return pl.pallas_call(
        functools.partial(section_kernel, tiles_here, merge, cols, rows, phi_count),
        out_shape=jax.ShapeDtypeStruct(x.shape, F32),
        in_specs=[anywhere] * len(operands),
        out_specs=anywhere,
        scratch_shapes=scratch,
        input_output_aliases=aliases,
        compiler_params=pltpu.CompilerParams(vmem_limit_bytes=SECTION_VMEM),
        cost_estimate=pl.CostEstimate(
            flops=SECTION_WEIGHT, bytes_accessed=8 * 2**20, transcendentals=2**17
        ),
        name=name,
    )(*operands)


def exchanged(x, axis, start):
    pairs = [(i, i + 1) for i in range(start, lax.axis_size(axis) - 1, 2)]
    return lax.ppermute(x, axis, pairs + [(j, i) for i, j in pairs])


def on_device(state, donor_base, fractions, dest_pos):
    x = state[0]
    fields, shells, cols, rows = x.shape
    tiles = lax.axis_size("tile")
    theta_step, phi_step, shell_step, spacing = geometry(rows, cols * tiles)
    dest = dest_pos[0, 0].T

    base, parts = donor_base[0, 0].T, jnp.swapaxes(fractions[0, 0], 1, 2)
    *ends, near, far = edges_call(x, dest)
    faces = (exchanged(ends[0], "rad", 0), exchanged(ends[1], "rad", 1))
    halos = (exchanged(near, "tile", 0), exchanged(far, "tile", 1))
    values = payload_call(x, base, parts)
    sent = gather_call(values, base, parts, *faces, tiles)

    colat = 0.25 * math.pi + (np.arange(rows) + 0.5) * theta_step
    peers = lax.axis_size("rad")
    radius = BASE_RADIUS + (np.arange(peers * shells) + 0.5) * shell_step
    every = np.zeros((peers, 8 + shells, LANES), np.float32)
    every[:, : rows // LANES] = (1.0 / np.sin(colat)).reshape(1, -1, LANES)
    every[:, 8:] = (1.0 / radius).reshape(peers, shells, 1)
    tables = jnp.asarray(every)
    last = rows // LANES - 1

    got = lax.all_to_all(sent, ("panel", "tile"), split_axis=0, concat_axis=0, tiled=True)
    new = section_call("inner", tuple(range(1, last)), tables, x, halos, faces)
    new = section_call("outer", (0, last), tables, x, halos, faces, (got, dest), new)
    return new[None]


def solution(mesh):
    placed = (
        P("panel", None, "rad", "tile", None),
        P("panel", "tile", None, None),
        P("panel", "tile", None, None, None),
        P("panel", "tile", None, None),
    )
    return jax.shard_map(
        on_device,
        mesh=mesh,
        in_specs=placed,
        out_specs=P("panel", None, "rad", "tile", None),
        check_vma=False,
    )
```

```python
import functools
import math

import jax
import jax.numpy as jnp
import numpy as np
from jax import lax
from jax.experimental import pallas as pl
from jax.experimental.pallas import tpu as pltpu
from jax.sharding import PartitionSpec as P

BASE_RADIUS = 0.6
F32 = jnp.float32
BF16 = jnp.bfloat16
LANES = 128
FIRST = 8
ROWS = 48
FACES_VMEM = 50 * 2**20
COLUMNS_VMEM = 60 * 2**20
PAYLOAD_VMEM = 50 * 2**20
SECTION_VMEM = 50 * 2**20
GATHER_VMEM = 50 * 2**20
SECTION_WEIGHT = 2 * 10**13
AHEAD = 4


def geometry(theta_count, phi_count):
    theta_step = 0.5 * math.pi / theta_count
    phi_step = 1.5 * math.pi / phi_count
    shell_step = 0.6 * min(theta_step, phi_step)
    corner = BASE_RADIUS * math.sin(0.25 * math.pi)
    spacing = min(shell_step, corner * theta_step, corner * phi_step)
    return (theta_step, phi_step, shell_step, spacing)


def halves(x):
    high = x.astype(BF16)
    return high, (x - high.astype(F32)).astype(BF16)


def lane_order(table):
    return jnp.concatenate([table[s : s + 1, :] for s in range(table.shape[0])], axis=1)


def turn(x):
    return jnp.transpose(jnp.concatenate([x] * (LANES // x.shape[0]), axis=0))


def stencils(base, fractions, cols, rows):
    base = lane_order(base)
    frac_theta = lane_order(fractions[0])
    frac_phi = lane_order(fractions[1])
    phi = base // rows
    theta = base - phi * rows
    position = lax.broadcasted_iota(jnp.int32, (rows, LANES), 0)
    along_theta = jnp.where(position == theta, 1.0 - frac_theta, 0.0)
    along_theta = along_theta + jnp.where(position == theta + 1, frac_theta, 0.0)
    place = lax.broadcasted_iota(jnp.int32, (cols, LANES), 0)
    along_phi = jnp.where(place == phi, 1.0 - frac_phi, 0.0)
    along_phi = along_phi + jnp.where(place == phi + 1, frac_phi, 0.0)
    return jnp.concatenate(halves(along_theta), axis=1), along_phi


def overset(block, both, along_phi):
    cols = along_phi.shape[0]
    x_high, x_low = halves(block)
    wide = jnp.dot(x_high, both, preferred_element_type=F32)
    low = jnp.dot(x_low, both[:, :LANES], preferred_element_type=F32)
    line = (wide[:, :LANES] + wide[:, LANES:] + low).reshape(-1, cols, LANES)
    return jnp.sum(line * along_phi[None], axis=1)


def faces_kernel(x_ref, near_ref, far_ref, sem):
    fields, shells, cols, rows = x_ref.shape
    upper = lax.rem(lax.axis_index("rad"), 2)
    copies = []
    for n, (ref, low) in enumerate(((near_ref, upper), (far_ref, 1 - upper))):
        s = (1 - low) * (shells - 1)
        for k in range(rows // LANES):
            copies.append(
                pltpu.make_async_copy(
                    x_ref.at[:, s, :, pl.ds(k * LANES, LANES)],
                    ref.at[pl.ds(k * fields, fields)],
                    sem.at[n, k],
                )
            )
    for copy in copies:
        copy.start()
    for copy in copies:
        copy.wait()


def faces_call(x):
    fields, shells, cols, rows = x.shape
    lane_tiles = rows // LANES
    anywhere = pl.BlockSpec(memory_space=pl.ANY)
    face = jax.ShapeDtypeStruct((lane_tiles * fields, cols, LANES), F32)
    return pl.pallas_call(
        faces_kernel,
        out_shape=(face, face),
        in_specs=[anywhere],
        out_specs=(anywhere,) * 2,
        scratch_shapes=[pltpu.SemaphoreType.DMA((2, lane_tiles))],
        compiler_params=pltpu.CompilerParams(vmem_limit_bytes=FACES_VMEM),
        cost_estimate=pl.CostEstimate(flops=10**6, bytes_accessed=2**21, transcendentals=0),
        name="faces",
    )(x)


def columns_kernel(x_ref, dest_ref, near_ref, far_ref, edges, dest_in, edge_sem, dest_sem, out_sem):
    fields, shells, cols, rows = x_ref.shape
    points = pltpu.make_async_copy(dest_ref, dest_in, dest_sem)
    points.start()
    sides = [
        pltpu.make_async_copy(
            x_ref.at[:, :, (0, cols - 2)[side] + c, :],
            edges.at[side, c, pl.ds(0, fields)],
            edge_sem.at[side, c],
        )
        for side in range(2)
        for c in range(2)
    ]
    second = lax.rem(lax.axis_index("tile"), 2)
    stores = [
        pltpu.make_async_copy(edges.at[1 - second], near_ref, out_sem.at[0]),
        pltpu.make_async_copy(edges.at[second], far_ref, out_sem.at[1]),
    ]
    for copy in sides:
        copy.start()
    points.wait()
    table = jnp.broadcast_to(lane_order(dest_in[...].astype(F32)), (shells, LANES))
    for side in range(2):
        edges[side, 0, fields, :, :LANES] = table
        edges[side, 1, fields] = jnp.zeros((shells, rows), F32)
    for copy in sides:
        copy.wait()
    for copy in stores:
        copy.start()
    for copy in stores:
        copy.wait()


def columns_call(x, dest):
    fields, shells, cols, rows = x.shape
    anywhere = pl.BlockSpec(memory_space=pl.ANY)
    edge = jax.ShapeDtypeStruct((2, fields + 1, shells, rows), F32)
    return pl.pallas_call(
        columns_kernel,
        out_shape=(edge, edge),
        in_specs=[anywhere] * 2,
        out_specs=(anywhere,) * 2,
        scratch_shapes=[
            pltpu.VMEM((2, *edge.shape), F32),
            pltpu.VMEM(dest.shape, dest.dtype),
            pltpu.SemaphoreType.DMA((2, 2)),
            pltpu.SemaphoreType.DMA,
            pltpu.SemaphoreType.DMA((2,)),
        ],
        compiler_params=pltpu.CompilerParams(vmem_limit_bytes=COLUMNS_VMEM),
        cost_estimate=pl.CostEstimate(flops=10**6, bytes_accessed=2**20, transcendentals=0),
        name="columns",
    )(x, dest)


def payload_kernel(
    x_ref, base_ref, frac_ref, values_ref, held, values, base_in, frac_in, load_sem, small_sem
):
    fields, shells, cols, rows = held.shape
    smalls = [
        pltpu.make_async_copy(ref, target, small_sem.at[n])
        for n, (ref, target) in enumerate(((base_ref, base_in), (frac_ref, frac_in)))
    ]

    def load(f):
        return pltpu.make_async_copy(x_ref.at[f], held.at[f], load_sem.at[f])

    for copy in smalls:
        copy.start()
    for f in range(AHEAD):
        load(f).start()
    for copy in smalls:
        copy.wait()
    both, along_phi = stencils(base_in[...], frac_in[...], cols, rows)
    for f in range(fields):
        load(f).wait()
        if f + AHEAD < fields:
            load(f + AHEAD).start()
        block = held[f].reshape(shells * cols, rows)
        values[f * shells : (f + 1) * shells, :] = overset(block, both, along_phi)
    last = pltpu.make_async_copy(values, values_ref, small_sem.at[0])
    last.start()
    last.wait()


def payload_call(x, base, fractions):
    fields, shells, cols, rows = x.shape
    anywhere = pl.BlockSpec(memory_space=pl.ANY)
    points = jax.ShapeDtypeStruct((fields * shells, LANES), F32)
    return pl.pallas_call(
        payload_kernel,
        out_shape=points,
        in_specs=[anywhere] * 3,
        out_specs=anywhere,
        scratch_shapes=[
            pltpu.VMEM(x.shape, F32),
            pltpu.VMEM(points.shape, F32),
            pltpu.VMEM(base.shape, base.dtype),
            pltpu.VMEM(fractions.shape, F32),
            pltpu.SemaphoreType.DMA((fields,)),
            pltpu.SemaphoreType.DMA((2,)),
        ],
        compiler_params=pltpu.CompilerParams(vmem_limit_bytes=PAYLOAD_VMEM),
        cost_estimate=pl.CostEstimate(flops=10**9, bytes_accessed=6 * 2**20, transcendentals=0),
        name="payload",
    )(x, base, fractions)


def gather_kernel(
    values_ref, base_ref, frac_ref, near_ref, far_ref, out_ref, values, base, frac, faces, sem
):
    cols = faces.shape[2]
    lane_tiles = faces.shape[1] // 8
    upper = lax.rem(lax.axis_index("rad"), 2)
    sources = (values_ref, base_ref, frac_ref, near_ref, far_ref)
    targets = (values, base, frac, faces.at[1 - upper], faces.at[upper])
    copies = [
        pltpu.make_async_copy(source, target, sem.at[n])
        for n, (source, target) in enumerate(zip(sources, targets))
    ]
    for copy in copies:
        copy.start()
    out_ref[...] = jnp.zeros(out_ref.shape, F32)
    tiles = out_ref.shape[0] // 16
    start = pl.multiple_of((1 - lax.axis_index("panel")) * (8 * tiles), 8 * tiles)
    for copy in copies[:3]:
        copy.wait()
    both, along_phi = stencils(base[...], frac[...], cols, lane_tiles * LANES)
    value = values[...]
    turned = turn(jnp.concatenate([value, pltpu.roll(value, 64, axis=1)], axis=0))
    row = lax.broadcasted_iota(jnp.int32, (tiles, LANES), 0)
    for n in range(2):
        own = turned[n * tiles : (n + 1) * tiles]
        before = jnp.where(row == 0, 0.0, pltpu.roll(own, 1, axis=0))
        after = jnp.where(row == tiles - 1, 0.0, pltpu.roll(own, tiles - 1, axis=0))
        for k, part in enumerate((own, before, after)):
            out_ref[pl.ds(start + (2 * k + n), tiles, stride=8), :] = part
    ends = []
    for copy in copies[3:]:
        copy.wait()
    for side in range(2):
        block = [
            faces[side, 8 * k : 8 * k + 8].reshape(8 * cols, LANES) for k in range(lane_tiles)
        ]
        ends.append(overset(jnp.concatenate(block, axis=1), both, along_phi))
    value = jnp.concatenate(ends, axis=0)
    parts = [value] + [pltpu.roll(value, LANES - tiles * s, axis=1) for s in range(1, 4)]
    turned = turn(jnp.concatenate(parts, axis=0))
    out_ref[pl.ds(start + 6, tiles, stride=8), :] = turned[:tiles]


def gather_call(values, base, fractions, near, far, tiles):
    vmem = pl.BlockSpec(memory_space=pltpu.VMEM)
    anywhere = pl.BlockSpec(memory_space=pl.ANY)
    return pl.pallas_call(
        gather_kernel,
        out_shape=jax.ShapeDtypeStruct((16 * tiles, LANES), F32),
        in_specs=[anywhere] * 5,
        out_specs=vmem,
        scratch_shapes=[
            pltpu.VMEM(values.shape, F32),
            pltpu.VMEM(base.shape, base.dtype),
            pltpu.VMEM(fractions.shape, F32),
            pltpu.VMEM((2, *near.shape), F32),
            pltpu.SemaphoreType.DMA((5,)),
        ],
        compiler_params=pltpu.CompilerParams(vmem_limit_bytes=GATHER_VMEM),
        cost_estimate=pl.CostEstimate(flops=10**6, bytes_accessed=2**18, transcendentals=0),
        name="gather",
    )(values, base, fractions, near, far)


def placed_points(got_ref, dest_ref, edge, split):
    tiles = got_ref.shape[0] // 8
    lane = lax.broadcasted_iota(jnp.int32, (64, LANES), 1)

    def rows(k):
        return got_ref[pl.ds(k, tiles, stride=8), :]

    def put(n, values, points):
        placing = jnp.where(
            lax.broadcasted_iota(jnp.int32, (LANES, LANES), 0) == points.astype(jnp.int32), 1.0, 0.0
        ).astype(BF16)
        dims = (((1,), (1,)), ((), ()))
        high, low = halves(values)
        count = values.shape[0]
        for part, value in enumerate((high, low)):
            split[n, part, :count, :] = lax.dot_general(
                value, placing, dims, preferred_element_type=F32
            )

    def tile_points(k):
        turned = turn(jnp.concatenate([rows(k), rows(k + 1)], axis=0))
        return jnp.where(lane < 64, turned[:64], turned[64:])

    own = lane_order(dest_ref[...].astype(F32))
    put(0, tile_points(0), own)
    turned = turn(rows(6))
    faces = turned[:16]
    for s in range(1, 4):
        faces = jnp.where(lane[:16] // tiles == s, turned[16 * s : 16 * s + 16], faces)
    put(1, faces, own)
    put(2, tile_points(2), edge[0])
    put(3, tile_points(4), edge[1])


def section_chunk(load, scale, lane):
    a_r, a_t, a_p, c_r, c_t, c_p = scale
    c_mid = 2.0 * c_r + 30.0 * c_t + 30.0 * c_p

    def parts(f, laplace=True):
        x = load(f, 0, 0, 0)
        left, right = load(f, 0, 0, -1), load(f, 0, 0, 1)
        inner, outer = load(f, -1, 0, 0), load(f, 1, 0, 0)
        t1 = pltpu.roll(jnp.where(lane < 1, right, x), LANES - 1, axis=1)
        t2 = pltpu.roll(jnp.where(lane < 2, right, x), LANES - 2, axis=1)
        s1 = pltpu.roll(jnp.where(lane >= LANES - 1, left, x), 1, axis=1)
        s2 = pltpu.roll(jnp.where(lane >= LANES - 2, left, x), 2, axis=1)
        p1, p2 = load(f, 0, 1, 0), load(f, 0, 2, 0)
        q1, q2 = load(f, 0, -1, 0), load(f, 0, -2, 0)
        g_r = outer - inner
        g_t = 8.0 * (t1 - s1) - (t2 - s2)
        g_p = 8.0 * (p1 - q1) - (p2 - q2)
        if not laplace:
            return x, g_r, g_t, g_p, None
        lap = c_r * (outer + inner) + c_t * (16.0 * (t1 + s1) - (t2 + s2))
        lap = lap + c_p * (16.0 * (p1 + q1) - (p2 + q2)) - c_mid * x
        return x, g_r, g_t, g_p, lap

    vel = tuple(load(1 + i, 0, 0, 0) * a for i, a in enumerate((a_r, a_t, a_p)))
    mag = tuple(load(4 + i, 0, 0, 0) * a for i, a in enumerate((a_r, a_t, a_p)))

    def along(v, g):
        return v[0] * g[0] + v[1] * g[1] + v[2] * g[2]

    new = [None] * 8
    rho, *g_rho, _ = parts(0, laplace=False)
    inv_rho = jnp.exp(-rho)
    rho_adv = along(vel, g_rho)
    pres, *g_pres, lap = parts(7)
    part_pres = pres - along(vel, g_pres) + 0.3 * lap
    div = None
    part_mag = []
    for i, a in enumerate((a_r, a_t, a_p)):
        u, *g_u, lap_u = parts(1 + i)
        b, *g_b, lap_b = parts(4 + i)
        term = a * g_u[i]
        div = term if div is None else div + term
        force = along(mag, g_b) - a * g_pres[i]
        new[1 + i] = u - along(vel, g_u) + inv_rho * force + 0.25 * lap_u
        part_mag.append((b, b - along(vel, g_b) + along(mag, g_u) + 0.2 * lap_b))
    for i, (b, part) in enumerate(part_mag):
        new[4 + i] = part - b * div
    new[0] = rho - rho_adv - div
    new[7] = part_pres - (5.0 / 3.0) * pres * div
    return new


def section_kernel(tiles_here, merge, cols, rows, phi_count, *refs):
    tables_ref, x_ref, near_ref, far_ref, near_face, far_face, *refs = refs
    fields, shells = x_ref.shape[:2]
    if merge:
        got_ref, dest_ref, _, *refs = refs
    out_ref, held, made, sides, tables, in_sem, halo_sem, small_sem, out_sem, *refs = refs
    if merge:
        got, dest, split, spread = refs
    lane_tiles = rows // LANES
    theta_step, phi_step, shell_step, spacing = geometry(rows, phi_count)
    step = 0.2 * spacing

    upper = lax.rem(lax.axis_index("rad"), 2)
    second = lax.rem(lax.axis_index("tile"), 2)

    def face(n):
        ref, side = ((near_face, 1 - upper), (far_face, upper))[n]
        at = pl.multiple_of(side * (shells + 1) * ROWS + FIRST, 8)
        return [
            pltpu.make_async_copy(
                ref.at[pl.ds(k * fields, fields)],
                held.at[k, :, pl.ds(at, cols), :],
                in_sem.at[n * (shells + 1), k],
            )
            for k in tiles_here
        ]

    def loads(s):
        return [
            pltpu.make_async_copy(
                x_ref.at[:, s, :, pl.ds(k * LANES, LANES)],
                held.at[k, :, pl.ds((s + 1) * ROWS + FIRST, cols), :],
                in_sem.at[s + 1, k],
            )
            for k in range(lane_tiles)
        ]

    def halo(n):
        ref, side = ((near_ref, 1 - second), (far_ref, second))[n]
        return pltpu.make_async_copy(ref, sides.at[side], halo_sem.at[n])

    def store(s, k):
        return pltpu.make_async_copy(
            made.at[k, s], out_ref.at[:, s, :, pl.ds(k * LANES, LANES)], out_sem.at[k, s]
        )

    slab = tables_ref.at[lax.axis_index("rad")]
    smalls = [pltpu.make_async_copy(slab, tables, small_sem.at[0])]
    if merge:
        start = pl.multiple_of((1 - lax.axis_index("panel")) * got.shape[0], got.shape[0])
        smalls.append(
            pltpu.make_async_copy(
                got_ref.at[pl.ds(start, got.shape[0])], got, small_sem.at[1]
            )
        )
        smalls.append(pltpu.make_async_copy(dest_ref, dest, small_sem.at[2]))
    for copy in smalls:
        copy.start()
    for side in range(2):
        halo(side).start()
    for copy in face(0) + face(1):
        copy.start()
    for s in range(AHEAD):
        for copy in loads(s):
            copy.start()
    for copy in smalls:
        copy.wait()

    lane = lax.broadcasted_iota(jnp.int32, (8, LANES), 1)

    for side in range(2):
        halo(side).wait()
    for side in range(2):
        for c in range(2):
            at = ROWS + (FIRST - 2, FIRST + cols)[side] + c
            for k in tiles_here:
                for f in range(fields):
                    held[k, f, pl.ds(at, shells, stride=ROWS), :] = sides[
                        side, c, f, :, k * LANES : (k + 1) * LANES
                    ]

    if merge:
        edge = [sides[side, 0, fields, 0:1, :LANES] for side in range(2)]
        placed_points(got, dest, edge, split)
        wide = lax.broadcasted_iota(jnp.int32, (LANES, LANES), 1)
        group = lax.broadcasted_iota(jnp.int32, (LANES, LANES), 0) // cols
        target = jnp.where(group < 2, group, LANES - 4 + group)
        spreading = jnp.where(wide == target, 1.0, 0.0).astype(BF16)
        row = lax.broadcasted_iota(jnp.int32, (8, LANES), 0)
        within = lane % cols

        def spread_rows(part, s, f, r):
            if isinstance(s, int) and s in (-1, shells):
                index = f if s == -1 else fields + f
                wanted, which = within == row + (8 * r - FIRST), 1
            else:
                index = f * shells + s
                if r == 0:
                    wanted, which = (row >= 6) & (within == row + (cols - 8)), 2
                elif r == ROWS // 8 - 1:
                    wanted, which = (row < 2) & (within == row), 3
                else:
                    wanted, which = within == row + (8 * r - FIRST), 0
            return jnp.where(wanted, split[which, part, pl.ds(index, 1), :], 0.0)

        def merge_shell(s):
            inside = not isinstance(s, int) or 0 <= s < shells
            tiles = range(ROWS // 8) if inside else range(1, ROWS // 8 - 1)
            for f in range(fields):
                for part in range(2):
                    block = [spread_rows(part, s, f, r) for r in tiles]
                    line = jnp.concatenate(block, axis=0).astype(BF16)
                    size = 8 * len(block)
                    spread[part, f * size : (f + 1) * size, :] = line
            total = fields * 8 * len(tiles)
            out = jnp.dot(spread[0, :total], spreading, preferred_element_type=F32)
            out = out + jnp.dot(spread[1, :total], spreading, preferred_element_type=F32)
            out = out.reshape(fields, len(tiles), 8, LANES)
            last = lane_tiles - 1
            for f in range(fields):
                for n, r in enumerate(tiles):
                    at = (f, pl.ds(pl.multiple_of((s + 1) * ROWS + 8 * r, 8), 8), slice(None))
                    block = out[f, n]
                    held[(0, *at)] = jnp.where(lane < 2, block, held[(0, *at)])
                    held[(last, *at)] = jnp.where(lane >= LANES - 2, block, held[(last, *at)])

    def compute(s, k):
        inverse = tables[pl.ds(8 + s, 1), :]
        over = tables[k : k + 1, :] * inverse

        def wide(row):
            return jnp.broadcast_to(row, (8, LANES))

        a_r = step * 0.5 / shell_step
        a_t = wide((step / (12.0 * theta_step)) * inverse)
        a_p = wide((step / (12.0 * phi_step)) * over)
        c_r = step * spacing / (shell_step * shell_step)
        c_t = wide((step * spacing / (12.0 * theta_step * theta_step)) * (inverse * inverse))
        c_p = wide((step * spacing / (12.0 * phi_step * phi_step)) * (over * over))

        for c in range(cols // 8):

            def load(f, ds, dc, dk):
                if not 0 <= k + dk < lane_tiles:
                    return jnp.zeros((8, LANES), F32)
                at = pl.multiple_of((s + 1 + ds) * ROWS + FIRST + 8 * c, 8)
                return held[k + dk, f, pl.ds(at + dc, 8), :]

            new = section_chunk(load, (a_r, a_t, a_p, c_r, c_t, c_p), lane)
            for f in range(fields):
                made[k, s, f, 8 * c : 8 * c + 8, :] = new[f]

        store(s, k).start()

    for copy in face(0) + face(1):
        copy.wait()
    if merge:
        merge_shell(-1)
        merge_shell(shells)

    @pl.loop(0, shells + 1)
    def _(t):
        @pl.when(t < shells)
        def _():
            @pl.when(t + AHEAD < shells)
            def _():
                for copy in loads(t + AHEAD):
                    copy.start()

            for copy in loads(t):
                copy.wait()
            if merge:
                merge_shell(t)

        @pl.when(t > 0)
        def _():
            for k in tiles_here:
                compute(t - 1, k)

    for s in range(shells):
        for k in tiles_here:
            store(s, k).wait()


def section_call(name, tiles_here, tables, x, halos, faces, found=(), before=None):
    fields, shells, cols, rows = x.shape
    lane_tiles = rows // LANES
    merge = before is not None
    anywhere = pl.BlockSpec(memory_space=pl.ANY)
    operands = [tables, x, *halos, *faces, *found]
    scratch = [
        pltpu.VMEM((lane_tiles, fields, (shells + 2) * ROWS, LANES), F32),
        pltpu.VMEM((lane_tiles, shells, fields, cols, LANES), F32),
        pltpu.VMEM((2, *halos[0].shape), F32),
        pltpu.VMEM(tables.shape[1:], F32),
        pltpu.SemaphoreType.DMA((shells + 2, lane_tiles)),
        pltpu.SemaphoreType.DMA((2,)),
        pltpu.SemaphoreType.DMA((3,)),
        pltpu.SemaphoreType.DMA((lane_tiles, shells)),
    ]
    aliases = {}
    if merge:
        aliases = {len(operands): 0}
        operands.append(before)
        got, dest = found
        scratch += [
            pltpu.VMEM((got.shape[0] // 2, LANES), F32),
            pltpu.VMEM(dest.shape, dest.dtype),
            pltpu.VMEM((4, 2, fields * shells, LANES), F32),
            pltpu.VMEM((2, fields * ROWS, LANES), BF16),
        ]
    phi_count = cols * lax.axis_size("tile")
    return pl.pallas_call(
        functools.partial(section_kernel, tiles_here, merge, cols, rows, phi_count),
        out_shape=jax.ShapeDtypeStruct(x.shape, F32),
        in_specs=[anywhere] * len(operands),
        out_specs=anywhere,
        scratch_shapes=scratch,
        input_output_aliases=aliases,
        compiler_params=pltpu.CompilerParams(vmem_limit_bytes=SECTION_VMEM),
        cost_estimate=pl.CostEstimate(
            flops=SECTION_WEIGHT, bytes_accessed=8 * 2**20, transcendentals=2**17
        ),
        name=name,
    )(*operands)


def exchanged(x, axis, start):
    pairs = [(i, i + 1) for i in range(start, lax.axis_size(axis) - 1, 2)]
    return lax.ppermute(x, axis, pairs + [(j, i) for i, j in pairs])


def on_device(state, donor_base, fractions, dest_pos):
    x = state[0]
    fields, shells, cols, rows = x.shape
    tiles = lax.axis_size("tile")
    theta_step, phi_step, shell_step, spacing = geometry(rows, cols * tiles)
    dest = dest_pos[0, 0].T

    base, parts = donor_base[0, 0].T, jnp.swapaxes(fractions[0, 0], 1, 2)
    ends = faces_call(x)
    faces = (exchanged(ends[0], "rad", 0), exchanged(ends[1], "rad", 1))
    near, far = columns_call(x, dest)
    halos = (exchanged(near, "tile", 0), exchanged(far, "tile", 1))
    values = payload_call(x, base, parts)
    sent = gather_call(values, base, parts, *faces, tiles)

    colat = 0.25 * math.pi + (np.arange(rows) + 0.5) * theta_step
    peers = lax.axis_size("rad")
    radius = BASE_RADIUS + (np.arange(peers * shells) + 0.5) * shell_step
    every = np.zeros((peers, 8 + shells, LANES), np.float32)
    every[:, : rows // LANES] = (1.0 / np.sin(colat)).reshape(1, -1, LANES)
    every[:, 8:] = (1.0 / radius).reshape(peers, shells, 1)
    tables = jnp.asarray(every)
    last = rows // LANES - 1

    got = lax.all_to_all(sent, ("panel", "tile"), split_axis=0, concat_axis=0, tiled=True)
    new = section_call("inner", tuple(range(1, last)), tables, x, halos, faces)
    new = section_call("outer", (0, last), tables, x, halos, faces, (got, dest), new)
    return new[None]


def solution(mesh):
    placed = (
        P("panel", None, "rad", "tile", None),
        P("panel", "tile", None, None),
        P("panel", "tile", None, None, None),
        P("panel", "tile", None, None),
    )
    return jax.shard_map(
        on_device,
        mesh=mesh,
        in_specs=placed,
        out_specs=P("panel", None, "rad", "tile", None),
        check_vma=False,
    )
```

```python
import functools
import math

import jax
import jax.numpy as jnp
import numpy as np
from jax import lax
from jax.experimental import pallas as pl
from jax.experimental.pallas import tpu as pltpu
from jax.sharding import PartitionSpec as P

BASE_RADIUS = 0.6
F32 = jnp.float32
BF16 = jnp.bfloat16
LANES = 128
FIRST = 8
ROWS = 48
FACES_VMEM = 50 * 2**20
COLUMNS_VMEM = 60 * 2**20
PAYLOAD_VMEM = 50 * 2**20
SECTION_VMEM = 50 * 2**20
GATHER_VMEM = 50 * 2**20
SECTION_WEIGHT = 2 * 10**13
AHEAD = 4


def geometry(theta_count, phi_count):
    theta_step = 0.5 * math.pi / theta_count
    phi_step = 1.5 * math.pi / phi_count
    shell_step = 0.6 * min(theta_step, phi_step)
    corner = BASE_RADIUS * math.sin(0.25 * math.pi)
    spacing = min(shell_step, corner * theta_step, corner * phi_step)
    return (theta_step, phi_step, shell_step, spacing)


def halves(x):
    high = x.astype(BF16)
    return high, (x - high.astype(F32)).astype(BF16)


def lane_order(table):
    return jnp.concatenate([table[s : s + 1, :] for s in range(table.shape[0])], axis=1)


def turn(x):
    return jnp.transpose(jnp.concatenate([x] * (LANES // x.shape[0]), axis=0))


def stencils(base, fractions, cols, rows):
    base = lane_order(base)
    frac_theta = lane_order(fractions[0])
    frac_phi = lane_order(fractions[1])
    phi = base // rows
    theta = base - phi * rows
    position = lax.broadcasted_iota(jnp.int32, (rows, LANES), 0)
    along_theta = jnp.where(position == theta, 1.0 - frac_theta, 0.0)
    along_theta = along_theta + jnp.where(position == theta + 1, frac_theta, 0.0)
    place = lax.broadcasted_iota(jnp.int32, (cols, LANES), 0)
    along_phi = jnp.where(place == phi, 1.0 - frac_phi, 0.0)
    along_phi = along_phi + jnp.where(place == phi + 1, frac_phi, 0.0)
    return jnp.concatenate(halves(along_theta), axis=1), along_phi


def overset(block, both, along_phi):
    cols = along_phi.shape[0]
    x_high, x_low = halves(block)
    wide = jnp.dot(x_high, both, preferred_element_type=F32)
    low = jnp.dot(x_low, both[:, :LANES], preferred_element_type=F32)
    line = (wide[:, :LANES] + wide[:, LANES:] + low).reshape(-1, cols, LANES)
    return jnp.sum(line * along_phi[None], axis=1)


def faces_kernel(x_ref, near_ref, far_ref, sem):
    fields, shells, cols, rows = x_ref.shape
    upper = lax.rem(lax.axis_index("rad"), 2)
    copies = []
    for n, (ref, low) in enumerate(((near_ref, upper), (far_ref, 1 - upper))):
        s = (1 - low) * (shells - 1)
        for k in range(rows // LANES):
            copies.append(
                pltpu.make_async_copy(
                    x_ref.at[:, s, :, pl.ds(k * LANES, LANES)],
                    ref.at[pl.ds(k * fields, fields)],
                    sem.at[n, k],
                )
            )
    for copy in copies:
        copy.start()
    for copy in copies:
        copy.wait()


def faces_call(x):
    fields, shells, cols, rows = x.shape
    lane_tiles = rows // LANES
    anywhere = pl.BlockSpec(memory_space=pl.ANY)
    face = jax.ShapeDtypeStruct((lane_tiles * fields, cols, LANES), F32)
    return pl.pallas_call(
        faces_kernel,
        out_shape=(face, face),
        in_specs=[anywhere],
        out_specs=(anywhere,) * 2,
        scratch_shapes=[pltpu.SemaphoreType.DMA((2, lane_tiles))],
        compiler_params=pltpu.CompilerParams(vmem_limit_bytes=FACES_VMEM),
        cost_estimate=pl.CostEstimate(flops=10**6, bytes_accessed=2**21, transcendentals=0),
        name="faces",
    )(x)


def columns_kernel(x_ref, dest_ref, near_ref, far_ref, edges, dest_in, edge_sem, dest_sem, out_sem):
    fields, shells, cols, rows = x_ref.shape
    points = pltpu.make_async_copy(dest_ref, dest_in, dest_sem)
    points.start()
    sides = [
        pltpu.make_async_copy(
            x_ref.at[:, :, (0, cols - 2)[side] + c, :],
            edges.at[side, c, pl.ds(0, fields)],
            edge_sem.at[side, c],
        )
        for side in range(2)
        for c in range(2)
    ]
    second = lax.rem(lax.axis_index("tile"), 2)
    stores = [
        pltpu.make_async_copy(edges.at[1 - second], near_ref, out_sem.at[0]),
        pltpu.make_async_copy(edges.at[second], far_ref, out_sem.at[1]),
    ]
    for copy in sides:
        copy.start()
    points.wait()
    table = jnp.broadcast_to(lane_order(dest_in[...].astype(F32)), (shells, LANES))
    for side in range(2):
        edges[side, 0, fields, :, :LANES] = table
        edges[side, 1, fields] = jnp.zeros((shells, rows), F32)
    for copy in sides:
        copy.wait()
    for copy in stores:
        copy.start()
    for copy in stores:
        copy.wait()


def columns_call(x, dest):
    fields, shells, cols, rows = x.shape
    anywhere = pl.BlockSpec(memory_space=pl.ANY)
    edge = jax.ShapeDtypeStruct((2, fields + 1, shells, rows), F32)
    return pl.pallas_call(
        columns_kernel,
        out_shape=(edge, edge),
        in_specs=[anywhere] * 2,
        out_specs=(anywhere,) * 2,
        scratch_shapes=[
            pltpu.VMEM((2, *edge.shape), F32),
            pltpu.VMEM(dest.shape, dest.dtype),
            pltpu.SemaphoreType.DMA((2, 2)),
            pltpu.SemaphoreType.DMA,
            pltpu.SemaphoreType.DMA((2,)),
        ],
        compiler_params=pltpu.CompilerParams(vmem_limit_bytes=COLUMNS_VMEM),
        cost_estimate=pl.CostEstimate(flops=10**6, bytes_accessed=2**20, transcendentals=0),
        name="columns",
    )(x, dest)


def payload_kernel(
    x_ref, base_ref, frac_ref, values_ref, held, values, base_in, frac_in, load_sem, small_sem
):
    fields, shells, cols, rows = held.shape
    smalls = [
        pltpu.make_async_copy(ref, target, small_sem.at[n])
        for n, (ref, target) in enumerate(((base_ref, base_in), (frac_ref, frac_in)))
    ]

    def load(f):
        return pltpu.make_async_copy(x_ref.at[f], held.at[f], load_sem.at[f])

    for copy in smalls:
        copy.start()
    for f in range(AHEAD):
        load(f).start()
    for copy in smalls:
        copy.wait()
    both, along_phi = stencils(base_in[...], frac_in[...], cols, rows)
    for f in range(fields):
        load(f).wait()
        if f + AHEAD < fields:
            load(f + AHEAD).start()
        block = held[f].reshape(shells * cols, rows)
        values[f * shells : (f + 1) * shells, :] = overset(block, both, along_phi)
    last = pltpu.make_async_copy(values, values_ref, small_sem.at[0])
    last.start()
    last.wait()


def payload_call(x, base, fractions):
    fields, shells, cols, rows = x.shape
    anywhere = pl.BlockSpec(memory_space=pl.ANY)
    points = jax.ShapeDtypeStruct((fields * shells, LANES), F32)
    return pl.pallas_call(
        payload_kernel,
        out_shape=points,
        in_specs=[anywhere] * 3,
        out_specs=anywhere,
        scratch_shapes=[
            pltpu.VMEM(x.shape, F32),
            pltpu.VMEM(points.shape, F32),
            pltpu.VMEM(base.shape, base.dtype),
            pltpu.VMEM(fractions.shape, F32),
            pltpu.SemaphoreType.DMA((fields,)),
            pltpu.SemaphoreType.DMA((2,)),
        ],
        compiler_params=pltpu.CompilerParams(vmem_limit_bytes=PAYLOAD_VMEM),
        cost_estimate=pl.CostEstimate(flops=10**9, bytes_accessed=6 * 2**20, transcendentals=0),
        name="payload",
    )(x, base, fractions)


def gather_kernel(
    values_ref, base_ref, frac_ref, near_ref, far_ref, out_ref, values, base, frac, faces, half, sem
):
    cols = faces.shape[2]
    lane_tiles = faces.shape[1] // 8
    upper = lax.rem(lax.axis_index("rad"), 2)
    sources = (values_ref, base_ref, frac_ref, near_ref, far_ref)
    targets = (values, base, frac, faces.at[1 - upper], faces.at[upper])
    copies = [
        pltpu.make_async_copy(source, target, sem.at[n])
        for n, (source, target) in enumerate(zip(sources, targets))
    ]
    for copy in copies:
        copy.start()
    size = half.shape[0]
    tiles = size // 8
    panel = lax.axis_index("panel")
    out_ref[pl.ds(pl.multiple_of(panel * size, size), size), :] = jnp.zeros(half.shape, F32)
    half[pl.ds(7, tiles, stride=8), :] = jnp.zeros((tiles, LANES), F32)
    for copy in copies[:3]:
        copy.wait()
    both, along_phi = stencils(base[...], frac[...], cols, lane_tiles * LANES)
    value = values[...]
    turned = turn(jnp.concatenate([value, pltpu.roll(value, 64, axis=1)], axis=0))
    row = lax.broadcasted_iota(jnp.int32, (tiles, LANES), 0)
    for n in range(2):
        own = turned[n * tiles : (n + 1) * tiles]
        before = jnp.where(row == 0, 0.0, pltpu.roll(own, 1, axis=0))
        after = jnp.where(row == tiles - 1, 0.0, pltpu.roll(own, tiles - 1, axis=0))
        for k, part in enumerate((own, before, after)):
            half[pl.ds(2 * k + n, tiles, stride=8), :] = part
    ends = []
    for copy in copies[3:]:
        copy.wait()
    for side in range(2):
        block = [
            faces[side, 8 * k : 8 * k + 8].reshape(8 * cols, LANES) for k in range(lane_tiles)
        ]
        ends.append(overset(jnp.concatenate(block, axis=1), both, along_phi))
    value = jnp.concatenate(ends, axis=0)
    parts = [value] + [pltpu.roll(value, LANES - tiles * s, axis=1) for s in range(1, 4)]
    turned = turn(jnp.concatenate(parts, axis=0))
    half[pl.ds(6, tiles, stride=8), :] = turned[:tiles]
    out_ref[pl.ds(pl.multiple_of((1 - panel) * size, size), size), :] = half[...]


def gather_call(values, base, fractions, near, far, tiles):
    vmem = pl.BlockSpec(memory_space=pltpu.VMEM)
    anywhere = pl.BlockSpec(memory_space=pl.ANY)
    return pl.pallas_call(
        gather_kernel,
        out_shape=jax.ShapeDtypeStruct((16 * tiles, LANES), F32),
        in_specs=[anywhere] * 5,
        out_specs=vmem,
        scratch_shapes=[
            pltpu.VMEM(values.shape, F32),
            pltpu.VMEM(base.shape, base.dtype),
            pltpu.VMEM(fractions.shape, F32),
            pltpu.VMEM((2, *near.shape), F32),
            pltpu.VMEM((8 * tiles, LANES), F32),
            pltpu.SemaphoreType.DMA((5,)),
        ],
        compiler_params=pltpu.CompilerParams(vmem_limit_bytes=GATHER_VMEM),
        cost_estimate=pl.CostEstimate(flops=10**6, bytes_accessed=2**18, transcendentals=0),
        name="gather",
    )(values, base, fractions, near, far)


def placed_points(got_ref, dest_ref, edge, split):
    tiles = got_ref.shape[0] // 8
    lane = lax.broadcasted_iota(jnp.int32, (64, LANES), 1)

    def rows(k):
        return got_ref[pl.ds(k, tiles, stride=8), :]

    def put(n, values, points):
        placing = jnp.where(
            lax.broadcasted_iota(jnp.int32, (LANES, LANES), 0) == points.astype(jnp.int32), 1.0, 0.0
        ).astype(BF16)
        dims = (((1,), (1,)), ((), ()))
        high, low = halves(values)
        count = values.shape[0]
        for part, value in enumerate((high, low)):
            split[n, part, :count, :] = lax.dot_general(
                value, placing, dims, preferred_element_type=F32
            )

    def tile_points(k):
        turned = turn(jnp.concatenate([rows(k), rows(k + 1)], axis=0))
        return jnp.where(lane < 64, turned[:64], turned[64:])

    own = lane_order(dest_ref[...].astype(F32))
    put(0, tile_points(0), own)
    turned = turn(rows(6))
    faces = turned[:16]
    for s in range(1, 4):
        faces = jnp.where(lane[:16] // tiles == s, turned[16 * s : 16 * s + 16], faces)
    put(1, faces, own)
    put(2, tile_points(2), edge[0])
    put(3, tile_points(4), edge[1])


def section_chunk(load, scale, lane):
    a_r, a_t, a_p, c_r, c_t, c_p = scale
    c_mid = 2.0 * c_r + 30.0 * c_t + 30.0 * c_p

    def parts(f, laplace=True):
        x = load(f, 0, 0, 0)
        left, right = load(f, 0, 0, -1), load(f, 0, 0, 1)
        inner, outer = load(f, -1, 0, 0), load(f, 1, 0, 0)
        t1 = pltpu.roll(jnp.where(lane < 1, right, x), LANES - 1, axis=1)
        t2 = pltpu.roll(jnp.where(lane < 2, right, x), LANES - 2, axis=1)
        s1 = pltpu.roll(jnp.where(lane >= LANES - 1, left, x), 1, axis=1)
        s2 = pltpu.roll(jnp.where(lane >= LANES - 2, left, x), 2, axis=1)
        p1, p2 = load(f, 0, 1, 0), load(f, 0, 2, 0)
        q1, q2 = load(f, 0, -1, 0), load(f, 0, -2, 0)
        g_r = outer - inner
        g_t = 8.0 * (t1 - s1) - (t2 - s2)
        g_p = 8.0 * (p1 - q1) - (p2 - q2)
        if not laplace:
            return x, g_r, g_t, g_p, None
        lap = c_r * (outer + inner) + c_t * (16.0 * (t1 + s1) - (t2 + s2))
        lap = lap + c_p * (16.0 * (p1 + q1) - (p2 + q2)) - c_mid * x
        return x, g_r, g_t, g_p, lap

    vel = tuple(load(1 + i, 0, 0, 0) * a for i, a in enumerate((a_r, a_t, a_p)))
    mag = tuple(load(4 + i, 0, 0, 0) * a for i, a in enumerate((a_r, a_t, a_p)))

    def along(v, g):
        return v[0] * g[0] + v[1] * g[1] + v[2] * g[2]

    new = [None] * 8
    rho, *g_rho, _ = parts(0, laplace=False)
    inv_rho = jnp.exp(-rho)
    rho_adv = along(vel, g_rho)
    pres, *g_pres, lap = parts(7)
    part_pres = pres - along(vel, g_pres) + 0.3 * lap
    div = None
    part_mag = []
    for i, a in enumerate((a_r, a_t, a_p)):
        u, *g_u, lap_u = parts(1 + i)
        b, *g_b, lap_b = parts(4 + i)
        term = a * g_u[i]
        div = term if div is None else div + term
        force = along(mag, g_b) - a * g_pres[i]
        new[1 + i] = u - along(vel, g_u) + inv_rho * force + 0.25 * lap_u
        part_mag.append((b, b - along(vel, g_b) + along(mag, g_u) + 0.2 * lap_b))
    for i, (b, part) in enumerate(part_mag):
        new[4 + i] = part - b * div
    new[0] = rho - rho_adv - div
    new[7] = part_pres - (5.0 / 3.0) * pres * div
    return new


def section_kernel(tiles_here, merge, cols, rows, phi_count, *refs):
    tables_ref, x_ref, near_ref, far_ref, near_face, far_face, *refs = refs
    fields, shells = x_ref.shape[:2]
    if merge:
        got_ref, dest_ref, _, *refs = refs
    out_ref, held, made, sides, tables, in_sem, halo_sem, small_sem, out_sem, *refs = refs
    if merge:
        got, dest, split, spread = refs
    lane_tiles = rows // LANES
    theta_step, phi_step, shell_step, spacing = geometry(rows, phi_count)
    step = 0.2 * spacing

    upper = lax.rem(lax.axis_index("rad"), 2)
    second = lax.rem(lax.axis_index("tile"), 2)

    def face(n):
        ref, side = ((near_face, 1 - upper), (far_face, upper))[n]
        at = pl.multiple_of(side * (shells + 1) * ROWS + FIRST, 8)
        return [
            pltpu.make_async_copy(
                ref.at[pl.ds(k * fields, fields)],
                held.at[k, :, pl.ds(at, cols), :],
                in_sem.at[n * (shells + 1), k],
            )
            for k in tiles_here
        ]

    def loads(s):
        return [
            pltpu.make_async_copy(
                x_ref.at[:, s, :, pl.ds(k * LANES, LANES)],
                held.at[k, :, pl.ds((s + 1) * ROWS + FIRST, cols), :],
                in_sem.at[s + 1, k],
            )
            for k in range(lane_tiles)
        ]

    def halo(n):
        ref, side = ((near_ref, 1 - second), (far_ref, second))[n]
        return pltpu.make_async_copy(ref, sides.at[side], halo_sem.at[n])

    def store(s, k):
        return pltpu.make_async_copy(
            made.at[k, s], out_ref.at[:, s, :, pl.ds(k * LANES, LANES)], out_sem.at[k, s]
        )

    slab = tables_ref.at[lax.axis_index("rad")]
    smalls = [pltpu.make_async_copy(slab, tables, small_sem.at[0])]
    if merge:
        start = pl.multiple_of((1 - lax.axis_index("panel")) * got.shape[0], got.shape[0])
        smalls.append(
            pltpu.make_async_copy(
                got_ref.at[pl.ds(start, got.shape[0])], got, small_sem.at[1]
            )
        )
        smalls.append(pltpu.make_async_copy(dest_ref, dest, small_sem.at[2]))
    for copy in smalls:
        copy.start()
    for side in range(2):
        halo(side).start()
    for copy in face(0) + face(1):
        copy.start()
    for s in range(AHEAD):
        for copy in loads(s):
            copy.start()
    for copy in smalls:
        copy.wait()

    lane = lax.broadcasted_iota(jnp.int32, (8, LANES), 1)

    for side in range(2):
        halo(side).wait()
    for side in range(2):
        for c in range(2):
            at = ROWS + (FIRST - 2, FIRST + cols)[side] + c
            for k in tiles_here:
                for f in range(fields):
                    held[k, f, pl.ds(at, shells, stride=ROWS), :] = sides[
                        side, c, f, :, k * LANES : (k + 1) * LANES
                    ]

    if merge:
        edge = [sides[side, 0, fields, 0:1, :LANES] for side in range(2)]
        placed_points(got, dest, edge, split)
        wide = lax.broadcasted_iota(jnp.int32, (LANES, LANES), 1)
        group = lax.broadcasted_iota(jnp.int32, (LANES, LANES), 0) // cols
        target = jnp.where(group < 2, group, LANES - 4 + group)
        spreading = jnp.where(wide == target, 1.0, 0.0).astype(BF16)
        row = lax.broadcasted_iota(jnp.int32, (8, LANES), 0)
        within = lane % cols

        def spread_rows(part, s, f, r):
            if isinstance(s, int) and s in (-1, shells):
                index = f if s == -1 else fields + f
                wanted, which = within == row + (8 * r - FIRST), 1
            else:
                index = f * shells + s
                if r == 0:
                    wanted, which = (row >= 6) & (within == row + (cols - 8)), 2
                elif r == ROWS // 8 - 1:
                    wanted, which = (row < 2) & (within == row), 3
                else:
                    wanted, which = within == row + (8 * r - FIRST), 0
            return jnp.where(wanted, split[which, part, pl.ds(index, 1), :], 0.0)

        def merge_shell(s):
            inside = not isinstance(s, int) or 0 <= s < shells
            tiles = range(ROWS // 8) if inside else range(1, ROWS // 8 - 1)
            for f in range(fields):
                for part in range(2):
                    block = [spread_rows(part, s, f, r) for r in tiles]
                    line = jnp.concatenate(block, axis=0).astype(BF16)
                    size = 8 * len(block)
                    spread[part, f * size : (f + 1) * size, :] = line
            total = fields * 8 * len(tiles)
            out = jnp.dot(spread[0, :total], spreading, preferred_element_type=F32)
            out = out + jnp.dot(spread[1, :total], spreading, preferred_element_type=F32)
            out = out.reshape(fields, len(tiles), 8, LANES)
            last = lane_tiles - 1
            for f in range(fields):
                for n, r in enumerate(tiles):
                    at = (f, pl.ds(pl.multiple_of((s + 1) * ROWS + 8 * r, 8), 8), slice(None))
                    block = out[f, n]
                    held[(0, *at)] = jnp.where(lane < 2, block, held[(0, *at)])
                    held[(last, *at)] = jnp.where(lane >= LANES - 2, block, held[(last, *at)])

    def compute(s, k):
        inverse = tables[pl.ds(8 + s, 1), :]
        over = tables[k : k + 1, :] * inverse

        def wide(row):
            return jnp.broadcast_to(row, (8, LANES))

        a_r = step * 0.5 / shell_step
        a_t = wide((step / (12.0 * theta_step)) * inverse)
        a_p = wide((step / (12.0 * phi_step)) * over)
        c_r = step * spacing / (shell_step * shell_step)
        c_t = wide((step * spacing / (12.0 * theta_step * theta_step)) * (inverse * inverse))
        c_p = wide((step * spacing / (12.0 * phi_step * phi_step)) * (over * over))

        for c in range(cols // 8):

            def load(f, ds, dc, dk):
                if not 0 <= k + dk < lane_tiles:
                    return jnp.zeros((8, LANES), F32)
                at = pl.multiple_of((s + 1 + ds) * ROWS + FIRST + 8 * c, 8)
                return held[k + dk, f, pl.ds(at + dc, 8), :]

            new = section_chunk(load, (a_r, a_t, a_p, c_r, c_t, c_p), lane)
            for f in range(fields):
                made[k, s, f, 8 * c : 8 * c + 8, :] = new[f]

        store(s, k).start()

    for copy in face(0) + face(1):
        copy.wait()
    if merge:
        merge_shell(-1)
        merge_shell(shells)

    @pl.loop(0, shells + 1)
    def _(t):
        @pl.when(t < shells)
        def _():
            @pl.when(t + AHEAD < shells)
            def _():
                for copy in loads(t + AHEAD):
                    copy.start()

            for copy in loads(t):
                copy.wait()
            if merge:
                merge_shell(t)

        @pl.when(t > 0)
        def _():
            for k in tiles_here:
                compute(t - 1, k)

    for s in range(shells):
        for k in tiles_here:
            store(s, k).wait()


def section_call(name, tiles_here, tables, x, halos, faces, found=(), before=None):
    fields, shells, cols, rows = x.shape
    lane_tiles = rows // LANES
    merge = before is not None
    anywhere = pl.BlockSpec(memory_space=pl.ANY)
    operands = [tables, x, *halos, *faces, *found]
    scratch = [
        pltpu.VMEM((lane_tiles, fields, (shells + 2) * ROWS, LANES), F32),
        pltpu.VMEM((lane_tiles, shells, fields, cols, LANES), F32),
        pltpu.VMEM((2, *halos[0].shape), F32),
        pltpu.VMEM(tables.shape[1:], F32),
        pltpu.SemaphoreType.DMA((shells + 2, lane_tiles)),
        pltpu.SemaphoreType.DMA((2,)),
        pltpu.SemaphoreType.DMA((3,)),
        pltpu.SemaphoreType.DMA((lane_tiles, shells)),
    ]
    aliases = {}
    if merge:
        aliases = {len(operands): 0}
        operands.append(before)
        got, dest = found
        scratch += [
            pltpu.VMEM((got.shape[0] // 2, LANES), F32),
            pltpu.VMEM(dest.shape, dest.dtype),
            pltpu.VMEM((4, 2, fields * shells, LANES), F32),
            pltpu.VMEM((2, fields * ROWS, LANES), BF16),
        ]
    phi_count = cols * lax.axis_size("tile")
    return pl.pallas_call(
        functools.partial(section_kernel, tiles_here, merge, cols, rows, phi_count),
        out_shape=jax.ShapeDtypeStruct(x.shape, F32),
        in_specs=[anywhere] * len(operands),
        out_specs=anywhere,
        scratch_shapes=scratch,
        input_output_aliases=aliases,
        compiler_params=pltpu.CompilerParams(vmem_limit_bytes=SECTION_VMEM),
        cost_estimate=pl.CostEstimate(
            flops=SECTION_WEIGHT, bytes_accessed=8 * 2**20, transcendentals=2**17
        ),
        name=name,
    )(*operands)


def exchanged(x, axis, start):
    pairs = [(i, i + 1) for i in range(start, lax.axis_size(axis) - 1, 2)]
    return lax.ppermute(x, axis, pairs + [(j, i) for i, j in pairs])


def on_device(state, donor_base, fractions, dest_pos):
    x = state[0]
    fields, shells, cols, rows = x.shape
    tiles = lax.axis_size("tile")
    theta_step, phi_step, shell_step, spacing = geometry(rows, cols * tiles)
    dest = dest_pos[0, 0].T

    base, parts = donor_base[0, 0].T, jnp.swapaxes(fractions[0, 0], 1, 2)
    ends = faces_call(x)
    faces = (exchanged(ends[0], "rad", 0), exchanged(ends[1], "rad", 1))
    near, far = columns_call(x, dest)
    halos = (exchanged(near, "tile", 0), exchanged(far, "tile", 1))
    values = payload_call(x, base, parts)
    sent = gather_call(values, base, parts, *faces, tiles)

    colat = 0.25 * math.pi + (np.arange(rows) + 0.5) * theta_step
    peers = lax.axis_size("rad")
    radius = BASE_RADIUS + (np.arange(peers * shells) + 0.5) * shell_step
    every = np.zeros((peers, 8 + shells, LANES), np.float32)
    every[:, : rows // LANES] = (1.0 / np.sin(colat)).reshape(1, -1, LANES)
    every[:, 8:] = (1.0 / radius).reshape(peers, shells, 1)
    tables = jnp.asarray(every)
    last = rows // LANES - 1

    got = lax.all_to_all(sent, ("panel", "tile"), split_axis=0, concat_axis=0, tiled=True)
    new = section_call("inner", tuple(range(1, last)), tables, x, halos, faces)
    new = section_call("outer", (0, last), tables, x, halos, faces, (got, dest), new)
    return new[None]


def solution(mesh):
    placed = (
        P("panel", None, "rad", "tile", None),
        P("panel", "tile", None, None),
        P("panel", "tile", None, None, None),
        P("panel", "tile", None, None),
    )
    return jax.shard_map(
        on_device,
        mesh=mesh,
        in_specs=placed,
        out_specs=P("panel", None, "rad", "tile", None),
        check_vma=False,
    )
```

```python
import functools
import math

import jax
import jax.numpy as jnp
import numpy as np
from jax import lax
from jax.experimental import pallas as pl
from jax.experimental.pallas import tpu as pltpu
from jax.sharding import PartitionSpec as P

BASE_RADIUS = 0.6
F32 = jnp.float32
BF16 = jnp.bfloat16
LANES = 128
FIRST = 8
ROWS = 48
FACES_VMEM = 50 * 2**20
COLUMNS_VMEM = 60 * 2**20
PAYLOAD_VMEM = 50 * 2**20
SECTION_VMEM = 50 * 2**20
GATHER_VMEM = 50 * 2**20
SECTION_WEIGHT = 2 * 10**13
AHEAD = 4


def geometry(theta_count, phi_count):
    theta_step = 0.5 * math.pi / theta_count
    phi_step = 1.5 * math.pi / phi_count
    shell_step = 0.6 * min(theta_step, phi_step)
    corner = BASE_RADIUS * math.sin(0.25 * math.pi)
    spacing = min(shell_step, corner * theta_step, corner * phi_step)
    return (theta_step, phi_step, shell_step, spacing)


def halves(x):
    high = x.astype(BF16)
    return high, (x - high.astype(F32)).astype(BF16)


def lane_order(table):
    return jnp.concatenate([table[s : s + 1, :] for s in range(table.shape[0])], axis=1)


def turn(x):
    return jnp.transpose(jnp.concatenate([x] * (LANES // x.shape[0]), axis=0))


def stencils(base, fractions, cols, rows):
    base = lane_order(base)
    frac_theta = lane_order(fractions[0])
    frac_phi = lane_order(fractions[1])
    phi = base // rows
    theta = base - phi * rows
    position = lax.broadcasted_iota(jnp.int32, (rows, LANES), 0)
    along_theta = jnp.where(position == theta, 1.0 - frac_theta, 0.0)
    along_theta = along_theta + jnp.where(position == theta + 1, frac_theta, 0.0)
    place = lax.broadcasted_iota(jnp.int32, (cols, LANES), 0)
    along_phi = jnp.where(place == phi, 1.0 - frac_phi, 0.0)
    along_phi = along_phi + jnp.where(place == phi + 1, frac_phi, 0.0)
    return jnp.concatenate(halves(along_theta), axis=1), along_phi


def overset(block, both, along_phi):
    cols = along_phi.shape[0]
    x_high, x_low = halves(block)
    wide = jnp.dot(x_high, both, preferred_element_type=F32)
    low = jnp.dot(x_low, both[:, :LANES], preferred_element_type=F32)
    line = (wide[:, :LANES] + wide[:, LANES:] + low).reshape(-1, cols, LANES)
    return jnp.sum(line * along_phi[None], axis=1)


def faces_kernel(x_ref, near_ref, far_ref, sem):
    fields, shells, cols, rows = x_ref.shape
    upper = lax.rem(lax.axis_index("rad"), 2)
    copies = []
    for n, (ref, low) in enumerate(((near_ref, upper), (far_ref, 1 - upper))):
        s = (1 - low) * (shells - 1)
        for k in range(rows // LANES):
            copies.append(
                pltpu.make_async_copy(
                    x_ref.at[:, s, :, pl.ds(k * LANES, LANES)],
                    ref.at[pl.ds(k * fields, fields)],
                    sem.at[n, k],
                )
            )
    for copy in copies:
        copy.start()
    for copy in copies:
        copy.wait()


def faces_call(x):
    fields, shells, cols, rows = x.shape
    lane_tiles = rows // LANES
    anywhere = pl.BlockSpec(memory_space=pl.ANY)
    face = jax.ShapeDtypeStruct((lane_tiles * fields, cols, LANES), F32)
    return pl.pallas_call(
        faces_kernel,
        out_shape=(face, face),
        in_specs=[anywhere],
        out_specs=(anywhere,) * 2,
        scratch_shapes=[pltpu.SemaphoreType.DMA((2, lane_tiles))],
        compiler_params=pltpu.CompilerParams(vmem_limit_bytes=FACES_VMEM),
        cost_estimate=pl.CostEstimate(flops=10**6, bytes_accessed=2**21, transcendentals=0),
        name="faces",
    )(x)


def columns_kernel(x_ref, dest_ref, near_ref, far_ref, edges, dest_in, edge_sem, dest_sem, out_sem):
    fields, shells, cols, rows = x_ref.shape
    points = pltpu.make_async_copy(dest_ref, dest_in, dest_sem)
    points.start()
    sides = [
        pltpu.make_async_copy(
            x_ref.at[:, :, (0, cols - 2)[side] + c, :],
            edges.at[side, c, pl.ds(0, fields)],
            edge_sem.at[side, c],
        )
        for side in range(2)
        for c in range(2)
    ]
    second = lax.rem(lax.axis_index("tile"), 2)
    stores = [
        pltpu.make_async_copy(edges.at[1 - second], near_ref, out_sem.at[0]),
        pltpu.make_async_copy(edges.at[second], far_ref, out_sem.at[1]),
    ]
    for copy in sides:
        copy.start()
    points.wait()
    table = jnp.broadcast_to(lane_order(dest_in[...].astype(F32)), (shells, LANES))
    for side in range(2):
        edges[side, 0, fields, :, :LANES] = table
        edges[side, 1, fields] = jnp.zeros((shells, rows), F32)
    for copy in sides:
        copy.wait()
    for copy in stores:
        copy.start()
    for copy in stores:
        copy.wait()


def columns_call(x, dest):
    fields, shells, cols, rows = x.shape
    anywhere = pl.BlockSpec(memory_space=pl.ANY)
    edge = jax.ShapeDtypeStruct((2, fields + 1, shells, rows), F32)
    return pl.pallas_call(
        columns_kernel,
        out_shape=(edge, edge),
        in_specs=[anywhere] * 2,
        out_specs=(anywhere,) * 2,
        scratch_shapes=[
            pltpu.VMEM((2, *edge.shape), F32),
            pltpu.VMEM(dest.shape, dest.dtype),
            pltpu.SemaphoreType.DMA((2, 2)),
            pltpu.SemaphoreType.DMA,
            pltpu.SemaphoreType.DMA((2,)),
        ],
        compiler_params=pltpu.CompilerParams(vmem_limit_bytes=COLUMNS_VMEM),
        cost_estimate=pl.CostEstimate(flops=10**6, bytes_accessed=2**20, transcendentals=0),
        name="columns",
    )(x, dest)


def payload_kernel(
    x_ref, base_ref, frac_ref, values_ref, held, values, base_in, frac_in, load_sem, small_sem
):
    fields, shells, cols, rows = held.shape
    smalls = [
        pltpu.make_async_copy(ref, target, small_sem.at[n])
        for n, (ref, target) in enumerate(((base_ref, base_in), (frac_ref, frac_in)))
    ]

    def load(f):
        return pltpu.make_async_copy(x_ref.at[f], held.at[f], load_sem.at[f])

    for copy in smalls:
        copy.start()
    for f in range(AHEAD):
        load(f).start()
    for copy in smalls:
        copy.wait()
    both, along_phi = stencils(base_in[...], frac_in[...], cols, rows)
    for f in range(fields):
        load(f).wait()
        if f + AHEAD < fields:
            load(f + AHEAD).start()
        block = held[f].reshape(shells * cols, rows)
        values[f * shells : (f + 1) * shells, :] = overset(block, both, along_phi)
    last = pltpu.make_async_copy(values, values_ref, small_sem.at[0])
    last.start()
    last.wait()


def payload_call(x, base, fractions):
    fields, shells, cols, rows = x.shape
    anywhere = pl.BlockSpec(memory_space=pl.ANY)
    points = jax.ShapeDtypeStruct((fields * shells, LANES), F32)
    return pl.pallas_call(
        payload_kernel,
        out_shape=points,
        in_specs=[anywhere] * 3,
        out_specs=anywhere,
        scratch_shapes=[
            pltpu.VMEM(x.shape, F32),
            pltpu.VMEM(points.shape, F32),
            pltpu.VMEM(base.shape, base.dtype),
            pltpu.VMEM(fractions.shape, F32),
            pltpu.SemaphoreType.DMA((fields,)),
            pltpu.SemaphoreType.DMA((2,)),
        ],
        compiler_params=pltpu.CompilerParams(vmem_limit_bytes=PAYLOAD_VMEM),
        cost_estimate=pl.CostEstimate(flops=10**9, bytes_accessed=6 * 2**20, transcendentals=0),
        name="payload",
    )(x, base, fractions)


def gather_kernel(
    values_ref, base_ref, frac_ref, near_ref, far_ref, out_ref, values, base, frac, faces, half, blank, sem
):
    cols = faces.shape[2]
    lane_tiles = faces.shape[1] // 8
    upper = lax.rem(lax.axis_index("rad"), 2)
    sources = (values_ref, base_ref, frac_ref, near_ref, far_ref)
    targets = (values, base, frac, faces.at[1 - upper], faces.at[upper])
    copies = [
        pltpu.make_async_copy(source, target, sem.at[n])
        for n, (source, target) in enumerate(zip(sources, targets))
    ]
    for copy in copies:
        copy.start()
    size = half.shape[0]
    tiles = size // 8
    panel = lax.axis_index("panel")
    blank[...] = jnp.zeros(blank.shape, F32)
    mine = pl.ds(pl.multiple_of(panel * size, size), size)
    other = pl.ds(pl.multiple_of((1 - panel) * size, size), size)
    empty = pltpu.make_async_copy(blank, out_ref.at[mine], sem.at[5])
    empty.start()
    half[pl.ds(7, tiles, stride=8), :] = jnp.zeros((tiles, LANES), F32)
    for copy in copies[:3]:
        copy.wait()
    both, along_phi = stencils(base[...], frac[...], cols, lane_tiles * LANES)
    value = values[...]
    turned = turn(jnp.concatenate([value, pltpu.roll(value, 64, axis=1)], axis=0))
    row = lax.broadcasted_iota(jnp.int32, (tiles, LANES), 0)
    for n in range(2):
        own = turned[n * tiles : (n + 1) * tiles]
        before = jnp.where(row == 0, 0.0, pltpu.roll(own, 1, axis=0))
        after = jnp.where(row == tiles - 1, 0.0, pltpu.roll(own, tiles - 1, axis=0))
        for k, part in enumerate((own, before, after)):
            half[pl.ds(2 * k + n, tiles, stride=8), :] = part
    ends = []
    for copy in copies[3:]:
        copy.wait()
    for side in range(2):
        block = [
            faces[side, 8 * k : 8 * k + 8].reshape(8 * cols, LANES) for k in range(lane_tiles)
        ]
        ends.append(overset(jnp.concatenate(block, axis=1), both, along_phi))
    value = jnp.concatenate(ends, axis=0)
    parts = [value] + [pltpu.roll(value, LANES - tiles * s, axis=1) for s in range(1, 4)]
    turned = turn(jnp.concatenate(parts, axis=0))
    half[pl.ds(6, tiles, stride=8), :] = turned[:tiles]
    full = pltpu.make_async_copy(half, out_ref.at[other], sem.at[6])
    full.start()
    empty.wait()
    full.wait()


def gather_call(values, base, fractions, near, far, tiles):
    anywhere = pl.BlockSpec(memory_space=pl.ANY)
    return pl.pallas_call(
        gather_kernel,
        out_shape=jax.ShapeDtypeStruct((16 * tiles, LANES), F32),
        in_specs=[anywhere] * 5,
        out_specs=anywhere,
        scratch_shapes=[
            pltpu.VMEM(values.shape, F32),
            pltpu.VMEM(base.shape, base.dtype),
            pltpu.VMEM(fractions.shape, F32),
            pltpu.VMEM((2, *near.shape), F32),
            pltpu.VMEM((8 * tiles, LANES), F32),
            pltpu.VMEM((8 * tiles, LANES), F32),
            pltpu.SemaphoreType.DMA((7,)),
        ],
        compiler_params=pltpu.CompilerParams(vmem_limit_bytes=GATHER_VMEM),
        cost_estimate=pl.CostEstimate(flops=10**6, bytes_accessed=2**18, transcendentals=0),
        name="gather",
    )(values, base, fractions, near, far)


def placed_points(got_ref, dest_ref, edge, split):
    tiles = got_ref.shape[0] // 8
    lane = lax.broadcasted_iota(jnp.int32, (64, LANES), 1)

    def rows(k):
        return got_ref[pl.ds(k, tiles, stride=8), :]

    def put(n, values, points):
        placing = jnp.where(
            lax.broadcasted_iota(jnp.int32, (LANES, LANES), 0) == points.astype(jnp.int32), 1.0, 0.0
        ).astype(BF16)
        dims = (((1,), (1,)), ((), ()))
        high, low = halves(values)
        count = values.shape[0]
        for part, value in enumerate((high, low)):
            split[n, part, :count, :] = lax.dot_general(
                value, placing, dims, preferred_element_type=F32
            )

    def tile_points(k):
        turned = turn(jnp.concatenate([rows(k), rows(k + 1)], axis=0))
        return jnp.where(lane < 64, turned[:64], turned[64:])

    own = lane_order(dest_ref[...].astype(F32))
    put(0, tile_points(0), own)
    turned = turn(rows(6))
    faces = turned[:16]
    for s in range(1, 4):
        faces = jnp.where(lane[:16] // tiles == s, turned[16 * s : 16 * s + 16], faces)
    put(1, faces, own)
    put(2, tile_points(2), edge[0])
    put(3, tile_points(4), edge[1])


def section_chunk(load, scale, lane):
    a_r, a_t, a_p, c_r, c_t, c_p = scale
    c_mid = 2.0 * c_r + 30.0 * c_t + 30.0 * c_p

    def parts(f, laplace=True):
        x = load(f, 0, 0, 0)
        left, right = load(f, 0, 0, -1), load(f, 0, 0, 1)
        inner, outer = load(f, -1, 0, 0), load(f, 1, 0, 0)
        t1 = pltpu.roll(jnp.where(lane < 1, right, x), LANES - 1, axis=1)
        t2 = pltpu.roll(jnp.where(lane < 2, right, x), LANES - 2, axis=1)
        s1 = pltpu.roll(jnp.where(lane >= LANES - 1, left, x), 1, axis=1)
        s2 = pltpu.roll(jnp.where(lane >= LANES - 2, left, x), 2, axis=1)
        p1, p2 = load(f, 0, 1, 0), load(f, 0, 2, 0)
        q1, q2 = load(f, 0, -1, 0), load(f, 0, -2, 0)
        g_r = outer - inner
        g_t = 8.0 * (t1 - s1) - (t2 - s2)
        g_p = 8.0 * (p1 - q1) - (p2 - q2)
        if not laplace:
            return x, g_r, g_t, g_p, None
        lap = c_r * (outer + inner) + c_t * (16.0 * (t1 + s1) - (t2 + s2))
        lap = lap + c_p * (16.0 * (p1 + q1) - (p2 + q2)) - c_mid * x
        return x, g_r, g_t, g_p, lap

    vel = tuple(load(1 + i, 0, 0, 0) * a for i, a in enumerate((a_r, a_t, a_p)))
    mag = tuple(load(4 + i, 0, 0, 0) * a for i, a in enumerate((a_r, a_t, a_p)))

    def along(v, g):
        return v[0] * g[0] + v[1] * g[1] + v[2] * g[2]

    new = [None] * 8
    rho, *g_rho, _ = parts(0, laplace=False)
    inv_rho = jnp.exp(-rho)
    rho_adv = along(vel, g_rho)
    pres, *g_pres, lap = parts(7)
    part_pres = pres - along(vel, g_pres) + 0.3 * lap
    div = None
    part_mag = []
    for i, a in enumerate((a_r, a_t, a_p)):
        u, *g_u, lap_u = parts(1 + i)
        b, *g_b, lap_b = parts(4 + i)
        term = a * g_u[i]
        div = term if div is None else div + term
        force = along(mag, g_b) - a * g_pres[i]
        new[1 + i] = u - along(vel, g_u) + inv_rho * force + 0.25 * lap_u
        part_mag.append((b, b - along(vel, g_b) + along(mag, g_u) + 0.2 * lap_b))
    for i, (b, part) in enumerate(part_mag):
        new[4 + i] = part - b * div
    new[0] = rho - rho_adv - div
    new[7] = part_pres - (5.0 / 3.0) * pres * div
    return new


def section_kernel(tiles_here, merge, cols, rows, phi_count, *refs):
    tables_ref, x_ref, near_ref, far_ref, near_face, far_face, *refs = refs
    fields, shells = x_ref.shape[:2]
    if merge:
        got_ref, dest_ref, _, *refs = refs
    out_ref, held, made, sides, tables, in_sem, halo_sem, small_sem, out_sem, *refs = refs
    if merge:
        got, dest, split, spread = refs
    lane_tiles = rows // LANES
    theta_step, phi_step, shell_step, spacing = geometry(rows, phi_count)
    step = 0.2 * spacing

    upper = lax.rem(lax.axis_index("rad"), 2)
    second = lax.rem(lax.axis_index("tile"), 2)

    def face(n):
        ref, side = ((near_face, 1 - upper), (far_face, upper))[n]
        at = pl.multiple_of(side * (shells + 1) * ROWS + FIRST, 8)
        return [
            pltpu.make_async_copy(
                ref.at[pl.ds(k * fields, fields)],
                held.at[k, :, pl.ds(at, cols), :],
                in_sem.at[n * (shells + 1), k],
            )
            for k in tiles_here
        ]

    def loads(s):
        return [
            pltpu.make_async_copy(
                x_ref.at[:, s, :, pl.ds(k * LANES, LANES)],
                held.at[k, :, pl.ds((s + 1) * ROWS + FIRST, cols), :],
                in_sem.at[s + 1, k],
            )
            for k in range(lane_tiles)
        ]

    def halo(n):
        ref, side = ((near_ref, 1 - second), (far_ref, second))[n]
        return pltpu.make_async_copy(ref, sides.at[side], halo_sem.at[n])

    def store(s, k):
        return pltpu.make_async_copy(
            made.at[k, s], out_ref.at[:, s, :, pl.ds(k * LANES, LANES)], out_sem.at[k, s]
        )

    slab = tables_ref.at[lax.axis_index("rad")]
    smalls = [pltpu.make_async_copy(slab, tables, small_sem.at[0])]
    if merge:
        start = pl.multiple_of((1 - lax.axis_index("panel")) * got.shape[0], got.shape[0])
        smalls.append(
            pltpu.make_async_copy(
                got_ref.at[pl.ds(start, got.shape[0])], got, small_sem.at[1]
            )
        )
        smalls.append(pltpu.make_async_copy(dest_ref, dest, small_sem.at[2]))
    for copy in smalls:
        copy.start()
    for side in range(2):
        halo(side).start()
    for copy in face(0) + face(1):
        copy.start()
    for s in range(AHEAD):
        for copy in loads(s):
            copy.start()
    for copy in smalls:
        copy.wait()

    lane = lax.broadcasted_iota(jnp.int32, (8, LANES), 1)

    for side in range(2):
        halo(side).wait()
    for side in range(2):
        for c in range(2):
            at = ROWS + (FIRST - 2, FIRST + cols)[side] + c
            for k in tiles_here:
                for f in range(fields):
                    held[k, f, pl.ds(at, shells, stride=ROWS), :] = sides[
                        side, c, f, :, k * LANES : (k + 1) * LANES
                    ]

    if merge:
        edge = [sides[side, 0, fields, 0:1, :LANES] for side in range(2)]
        placed_points(got, dest, edge, split)
        wide = lax.broadcasted_iota(jnp.int32, (LANES, LANES), 1)
        group = lax.broadcasted_iota(jnp.int32, (LANES, LANES), 0) // cols
        target = jnp.where(group < 2, group, LANES - 4 + group)
        spreading = jnp.where(wide == target, 1.0, 0.0).astype(BF16)
        row = lax.broadcasted_iota(jnp.int32, (8, LANES), 0)
        within = lane % cols

        def spread_rows(part, s, f, r):
            if isinstance(s, int) and s in (-1, shells):
                index = f if s == -1 else fields + f
                wanted, which = within == row + (8 * r - FIRST), 1
            else:
                index = f * shells + s
                if r == 0:
                    wanted, which = (row >= 6) & (within == row + (cols - 8)), 2
                elif r == ROWS // 8 - 1:
                    wanted, which = (row < 2) & (within == row), 3
                else:
                    wanted, which = within == row + (8 * r - FIRST), 0
            return jnp.where(wanted, split[which, part, pl.ds(index, 1), :], 0.0)

        def merge_shell(s):
            inside = not isinstance(s, int) or 0 <= s < shells
            tiles = range(ROWS // 8) if inside else range(1, ROWS // 8 - 1)
            for f in range(fields):
                for part in range(2):
                    block = [spread_rows(part, s, f, r) for r in tiles]
                    line = jnp.concatenate(block, axis=0).astype(BF16)
                    size = 8 * len(block)
                    spread[part, f * size : (f + 1) * size, :] = line
            total = fields * 8 * len(tiles)
            out = jnp.dot(spread[0, :total], spreading, preferred_element_type=F32)
            out = out + jnp.dot(spread[1, :total], spreading, preferred_element_type=F32)
            out = out.reshape(fields, len(tiles), 8, LANES)
            last = lane_tiles - 1
            for f in range(fields):
                for n, r in enumerate(tiles):
                    at = (f, pl.ds(pl.multiple_of((s + 1) * ROWS + 8 * r, 8), 8), slice(None))
                    block = out[f, n]
                    held[(0, *at)] = jnp.where(lane < 2, block, held[(0, *at)])
                    held[(last, *at)] = jnp.where(lane >= LANES - 2, block, held[(last, *at)])

    def compute(s, k):
        inverse = tables[pl.ds(8 + s, 1), :]
        over = tables[k : k + 1, :] * inverse

        def wide(row):
            return jnp.broadcast_to(row, (8, LANES))

        a_r = step * 0.5 / shell_step
        a_t = wide((step / (12.0 * theta_step)) * inverse)
        a_p = wide((step / (12.0 * phi_step)) * over)
        c_r = step * spacing / (shell_step * shell_step)
        c_t = wide((step * spacing / (12.0 * theta_step * theta_step)) * (inverse * inverse))
        c_p = wide((step * spacing / (12.0 * phi_step * phi_step)) * (over * over))

        for c in range(cols // 8):

            def load(f, ds, dc, dk):
                if not 0 <= k + dk < lane_tiles:
                    return jnp.zeros((8, LANES), F32)
                at = pl.multiple_of((s + 1 + ds) * ROWS + FIRST + 8 * c, 8)
                return held[k + dk, f, pl.ds(at + dc, 8), :]

            new = section_chunk(load, (a_r, a_t, a_p, c_r, c_t, c_p), lane)
            for f in range(fields):
                made[k, s, f, 8 * c : 8 * c + 8, :] = new[f]

        store(s, k).start()

    for copy in face(0) + face(1):
        copy.wait()
    if merge:
        merge_shell(-1)
        merge_shell(shells)

    @pl.loop(0, shells + 1)
    def _(t):
        @pl.when(t < shells)
        def _():
            @pl.when(t + AHEAD < shells)
            def _():
                for copy in loads(t + AHEAD):
                    copy.start()

            for copy in loads(t):
                copy.wait()
            if merge:
                merge_shell(t)

        @pl.when(t > 0)
        def _():
            for k in tiles_here:
                compute(t - 1, k)

    for s in range(shells):
        for k in tiles_here:
            store(s, k).wait()


def section_call(name, tiles_here, tables, x, halos, faces, found=(), before=None):
    fields, shells, cols, rows = x.shape
    lane_tiles = rows // LANES
    merge = before is not None
    anywhere = pl.BlockSpec(memory_space=pl.ANY)
    operands = [tables, x, *halos, *faces, *found]
    scratch = [
        pltpu.VMEM((lane_tiles, fields, (shells + 2) * ROWS, LANES), F32),
        pltpu.VMEM((lane_tiles, shells, fields, cols, LANES), F32),
        pltpu.VMEM((2, *halos[0].shape), F32),
        pltpu.VMEM(tables.shape[1:], F32),
        pltpu.SemaphoreType.DMA((shells + 2, lane_tiles)),
        pltpu.SemaphoreType.DMA((2,)),
        pltpu.SemaphoreType.DMA((3,)),
        pltpu.SemaphoreType.DMA((lane_tiles, shells)),
    ]
    aliases = {}
    if merge:
        aliases = {len(operands): 0}
        operands.append(before)
        got, dest = found
        scratch += [
            pltpu.VMEM((got.shape[0] // 2, LANES), F32),
            pltpu.VMEM(dest.shape, dest.dtype),
            pltpu.VMEM((4, 2, fields * shells, LANES), F32),
            pltpu.VMEM((2, fields * ROWS, LANES), BF16),
        ]
    phi_count = cols * lax.axis_size("tile")
    return pl.pallas_call(
        functools.partial(section_kernel, tiles_here, merge, cols, rows, phi_count),
        out_shape=jax.ShapeDtypeStruct(x.shape, F32),
        in_specs=[anywhere] * len(operands),
        out_specs=anywhere,
        scratch_shapes=scratch,
        input_output_aliases=aliases,
        compiler_params=pltpu.CompilerParams(vmem_limit_bytes=SECTION_VMEM),
        cost_estimate=pl.CostEstimate(
            flops=SECTION_WEIGHT, bytes_accessed=8 * 2**20, transcendentals=2**17
        ),
        name=name,
    )(*operands)


def exchanged(x, axis, start):
    pairs = [(i, i + 1) for i in range(start, lax.axis_size(axis) - 1, 2)]
    return lax.ppermute(x, axis, pairs + [(j, i) for i, j in pairs])


def on_device(state, donor_base, fractions, dest_pos):
    x = state[0]
    fields, shells, cols, rows = x.shape
    tiles = lax.axis_size("tile")
    theta_step, phi_step, shell_step, spacing = geometry(rows, cols * tiles)
    dest = dest_pos[0, 0].T

    base, parts = donor_base[0, 0].T, jnp.swapaxes(fractions[0, 0], 1, 2)
    ends = faces_call(x)
    faces = (exchanged(ends[0], "rad", 0), exchanged(ends[1], "rad", 1))
    near, far = columns_call(x, dest)
    halos = (exchanged(near, "tile", 0), exchanged(far, "tile", 1))
    values = payload_call(x, base, parts)
    sent = gather_call(values, base, parts, *faces, tiles)

    colat = 0.25 * math.pi + (np.arange(rows) + 0.5) * theta_step
    peers = lax.axis_size("rad")
    radius = BASE_RADIUS + (np.arange(peers * shells) + 0.5) * shell_step
    every = np.zeros((peers, 8 + shells, LANES), np.float32)
    every[:, : rows // LANES] = (1.0 / np.sin(colat)).reshape(1, -1, LANES)
    every[:, 8:] = (1.0 / radius).reshape(peers, shells, 1)
    tables = jnp.asarray(every)
    last = rows // LANES - 1

    got = lax.all_to_all(sent, ("panel", "tile"), split_axis=0, concat_axis=0, tiled=True)
    new = section_call("inner", tuple(range(1, last)), tables, x, halos, faces)
    new = section_call("outer", (0, last), tables, x, halos, faces, (got, dest), new)
    return new[None]


def solution(mesh):
    placed = (
        P("panel", None, "rad", "tile", None),
        P("panel", "tile", None, None),
        P("panel", "tile", None, None, None),
        P("panel", "tile", None, None),
    )
    return jax.shard_map(
        on_device,
        mesh=mesh,
        in_specs=placed,
        out_specs=P("panel", None, "rad", "tile", None),
        check_vma=False,
    )
```
